256 devices in a mesh: row: 32 (over z_lo, y, x), col: 8 (over z_hi, core).
Axes of the slice: x: 4, y: 4, z: 8 (z_hi: 4, z_lo: 2; z = z_hi * 2 + z_lo), core: 2. Of those that a mesh axis runs over, the one named last changes fastest.
Arguments:
- latent: bfloat16 [12288, 512], P('row', 'col'), may hold values from -6 to 6
- w_kv: bfloat16 [512, 8192], P('row', 'col'), may hold values from -0.25 to 0.25
- queries: bfloat16 [12288, 4096], P('row', 'col'), may hold values from -240 to 240
- w_out: bfloat16 [4096, 7168], P('row', 'col'), may hold values from -0.09375 to 0.09375
Outputs:
- mixed: bfloat16 [12288, 7168], P('row', 'col')
The draws below stay inside these ranges and needn't reach their ends.
All inputs are finite; a program needn't handle non-finite values.
Results may differ from the reference program's by a relative error of at most 0.012.
The reference program's roundings to bfloat16 on the way (of `key_values`, `weights` and `attended`) count: a program that leaves them out, or rounds other values in their place, can miss the bound.
Values may be sent and summed in bfloat16 or wider, within the bound.
A program may use at most 128 MiB of HBM per device.

```python
import math
import jax
import jax.numpy as jnp
from jax import lax

D = 7168
HEADS = 32
HEAD = 128
LATENT = 512
TOKENS = 12288


def draw_queries(key, part):
    first = jax.random.fold_in(jax.random.fold_in(key, 17), 0)
    values = jnp.clip(jax.random.normal(first, (TOKENS, HEADS * HEAD), jnp.float32), -4.0, 4.0)
    return values.astype(jnp.bfloat16)


def shard_levels(key, extent, pieces, smallest, top_value):
    def one(dim, blocks):
        draws = jax.random.uniform(jax.random.fold_in(jax.random.fold_in(key, 6), dim), (blocks,), jnp.float32, smallest / len(pieces), top_value / len(pieces))
        return jnp.repeat(jnp.exp(draws), extent[dim] // blocks).reshape((-1,) + (1,) * (len(extent) - dim - 1))

    factor_of = one(*pieces[0])
    for cut in pieces[1:]:
        factor_of = factor_of * one(*cut)
    return factor_of


def gaussian(own_key, extent, scale, limit, shards=(), held_as=jnp.bfloat16):
    result = jax.random.normal(own_key, extent, jnp.float32) * scale
    if len(shards) > 0:
        result = shard_levels(own_key, extent, shards, -0.22, 0.18) * result
    return jnp.clip(result, min=-limit, max=limit).astype(held_as)


def setup_inputs(seed: int = 0) -> dict:
    seeds = jax.random.split(jax.random.key(seed), 5)
    latent = gaussian(seeds[0], (TOKENS, LATENT), 1.0, 6.0, ((0, 32), (1, 8)))
    w_kv = gaussian(seeds[1], (LATENT, 2 * HEADS * HEAD), LATENT ** -0.5, 0.25, ((0, 32), (1, 8)))
    queries = draw_queries(jax.random.fold_in(seeds[4], 71), 0)
    w_out = gaussian(seeds[3], (HEADS * HEAD, D), (HEADS * HEAD) ** -0.5, 0.09375, ((0, 32), (1, 8)))
    return {"latent": latent, "w_kv": w_kv, "queries": queries, "w_out": w_out}


NEG_FILL = -1e30


def reference(latent, w_kv, queries, w_out):
    key_values = jnp.dot(latent, w_kv, preferred_element_type=jnp.float32).astype(jnp.bfloat16)
    key_values = key_values.reshape(TOKENS, HEADS, 2 * HEAD).transpose(1, 0, 2)
    head_queries = queries.reshape(TOKENS, HEADS, HEAD).transpose(1, 0, 2)
    block_rows = math.gcd(TOKENS, 1024)
    score_scale = HEAD ** -0.5
    key_pos = jnp.arange(TOKENS, dtype=jnp.int32)

    def one_head(operands):
        query_head, pairs = operands
        keys_only = pairs[:, :HEAD]
        values_only = pairs[:, HEAD:]

        def one_block(first_row):
            query_block = lax.dynamic_slice_in_dim(query_head, first_row, block_rows, 0)
            scores = lax.dot_general(query_block, keys_only, (((1,), (1,)), ((), ())), preferred_element_type=jnp.float32) * score_scale
            query_pos = first_row + jnp.arange(block_rows, dtype=jnp.int32)
            allowed = key_pos[None, :] <= query_pos[:, None]
            scores = jnp.where(allowed, scores, NEG_FILL)
            highest = jnp.max(scores, axis=1, keepdims=True)
            weights = jnp.where(allowed, jnp.exp(scores - highest), 0.0)
            totals = jnp.sum(weights, axis=1, keepdims=True)
            summed = jnp.dot(weights.astype(jnp.bfloat16), values_only, preferred_element_type=jnp.float32)
            return (summed / totals).astype(jnp.bfloat16)

        starts = jnp.arange(TOKENS // block_rows, dtype=jnp.int32) * block_rows
        return lax.map(one_block, starts).reshape(TOKENS, HEAD)

    attended = lax.map(one_head, (head_queries, key_values))
    attended = attended.transpose(1, 0, 2).reshape(TOKENS, HEADS * HEAD)
    return jnp.dot(attended, w_out, preferred_element_type=jnp.float32).astype(jnp.bfloat16)
```

```python
import functools

import jax
import jax.numpy as jnp
from jax import lax
from jax.experimental import pallas as pl
from jax.experimental.pallas import tpu as pltpu
from jax.sharding import PartitionSpec as P

HEAD = 128
NEG_FILL = -1e30
MESH = pl.DeviceIdType.MESH
BF16 = jnp.bfloat16
F32 = jnp.float32

ROWS = 32
TOK = 384
STRIPE = 48
QROWS = 4
QB = QROWS * STRIPE
KB = QROWS * TOK
BLOCKS = ROWS // QROWS
SCALE = HEAD**-0.5 * 1.4426950408889634


def kernel(
    lat_ref, wkv_ref, q_ref, wout_ref, out_ref,
    pieces, lat, wkv, wkt, queries, keys_t, values, att, feats, wout, acc, top, total,
    cs, cr, qs, qr, ws, wr, gs, gr, ss, sr, os, orr, hs, hr, zs, zr, ls,
):
    row = lax.axis_index("row")
    col = lax.axis_index("col")
    x = lax.rem(row, 4)
    y = lax.rem(row // 4, 4)
    zl = row // 16
    zh = col // 2
    core = lax.rem(col, 2)
    sibling = (row, zh * 2 + 1 - core)

    def row_of(xx, yy, zz):
        return zz * 16 + yy * 4 + xx

    def up(v):
        return lax.rem(v + 1, 4)

    def down(v):
        return lax.rem(v + 3, 4)

    def across(v):
        return lax.rem(v + 2, 4)

    def remote(src, dst, send, recv, device):
        return pltpu.make_async_remote_copy(
            src_ref=src, dst_ref=dst, send_sem=send, recv_sem=recv,
            device_id=device, device_id_type=MESH,
        )

    barrier = pltpu.get_barrier_semaphore()

    def greet_row(d, carry):
        pl.semaphore_signal(
            barrier, inc=1, device_id=(lax.rem(row + d, ROWS), col), device_id_type=MESH
        )
        return carry

    def greet_col(d, carry):
        pl.semaphore_signal(
            barrier, inc=1, device_id=(row, lax.rem(col + d, 8)), device_id_type=MESH
        )
        return carry

    lax.fori_loop(1, 8, greet_col, 0)
    lax.fori_loop(1, ROWS, greet_row, 0)
    pl.semaphore_wait(barrier, ROWS - 1 + 7)

    home = zh // 2
    own_slot = lax.rem(zh, 2) * 2 + core

    def col_copy(d):
        dst = (row, lax.rem(zh + d, 4) * 2 + home)
        return remote(lat_ref, pieces.at[own_slot], cs.at[d], cr.at[own_slot], dst)

    for d in (2, 1, 3):
        col_copy(d).start()

    @pl.when(core != home)
    def _():
        col_copy(0).start()

    own_piece = pltpu.make_async_copy(lat_ref, pieces.at[own_slot], ls.at[0])

    @pl.when(core == home)
    def _():
        own_piece.start()

    head_local = x

    def q_copy(d):
        peer = lax.rem(row + d, ROWS)
        part = q_ref.at[
            pl.ds(pl.multiple_of(peer // 4 * STRIPE, STRIPE), STRIPE),
            pl.ds(pl.multiple_of(lax.rem(peer, 4) * HEAD, HEAD), HEAD),
        ]
        return part, remote(part, queries.at[row], qs.at[d], qr.at[d], (peer, col))

    def w_copy(d):
        peer = lax.rem(row + d, ROWS)
        part = wkv_ref.at[:, pl.ds(pl.multiple_of(lax.rem(peer, 4) * 256, 256), 256)]
        return part, remote(part, wkv.at[row], ws.at[d], wr.at[d], (peer, col))

    def small_start(d, carry):
        w_copy(d)[1].start()
        q_copy(d)[1].start()
        return carry

    lax.fori_loop(1, ROWS, small_start, 0)
    local_q = pltpu.make_async_copy(q_copy(0)[0], queries.at[row], ls.at[1])
    local_w = pltpu.make_async_copy(w_copy(0)[0], wkv.at[row], ls.at[2])
    local_q.start()
    local_w.start()

    def axes(half):
        if half == 0:
            return x, y, lambda aa, bb, zz: row_of(aa, bb, zz)
        return y, x, lambda aa, bb, zz: row_of(bb, aa, zz)

    def lat_copy(half, n):
        a, b, dev = axes(half)
        buf = lat.at[core * 2 + half]

        def at(aa, bb, zz, count):
            return buf.at[pl.ds((aa * 4 + bb) * 2 + zz, count)]

        if n == 0:
            src, to = at(a, b, zl, 1), dev(a, b, 1 - zl)
        elif n == 1:
            src, to = at(a, b, 0, 2), dev(a, up(b), zl)
        elif n == 2:
            src, to = at(a, b, 0, 2), dev(a, down(b), zl)
        elif n == 3:
            src, to = at(a, down(b), 0, 1), dev(a, up(b), zl)
        elif n == 4:
            src, to = at(a, up(b), 1, 1), dev(a, down(b), zl)
        elif n == 5:
            src, to = at(a, 0, 0, 8), dev(up(a), b, zl)
        elif n == 6:
            src, to = at(a, 0, 0, 8), dev(down(a), b, zl)
        elif n == 7:
            src, to = at(down(a), 0, 0, 4), dev(up(a), b, zl)
        else:
            src, to = at(up(a), 2, 0, 4), dev(down(a), b, zl)
        return remote(src, src, gs.at[half, n], gr.at[half, n], (to, col))

    def sib_copy(half, n):
        a, _, _ = axes(half)
        group = (a, down(a), up(a), across(a))[n]
        src = lat.at[core * 2 + half, pl.ds(group * 8, 8)]
        return remote(src, src, ss.at[half, n], sr.at[half, n], sibling)

    def out_copy(half, n):
        a, b, dev = axes(half)
        buf = wout.at[half]
        if n == 1 or n == 2:
            src = buf.at[a * 4 + b]
            to = dev(a, up(b) if n == 1 else down(b), zl)
        elif n == 3:
            src, to = buf.at[a * 4 + down(b), pl.ds(0, 64)], dev(a, up(b), zl)
        elif n == 4:
            src, to = buf.at[a * 4 + up(b), pl.ds(64, 64)], dev(a, down(b), zl)
        elif n == 5 or n == 6:
            src = buf.at[pl.ds(a * 4, 4)]
            to = dev(up(a) if n == 5 else down(a), b, zl)
        elif n == 7:
            src, to = buf.at[pl.ds(down(a) * 4, 2)], dev(up(a), b, zl)
        else:
            src, to = buf.at[pl.ds(up(a) * 4 + 2, 2)], dev(down(a), b, zl)
        return remote(src, src, os.at[half, n], orr.at[half, n], (to, col))

    own_out = wout.at[zl, jnp.where(zl == 0, x * 4 + y, y * 4 + x)]
    out_first = remote(wout_ref, own_out, os.at[0, 0], orr.at[0, 0], (row_of(x, y, 1 - zl), col))
    out_local = pltpu.make_async_copy(wout_ref, own_out, ls.at[3])

    @pl.when(core != home)
    def _():
        col_copy(0).wait_send()

    @pl.when(core == home)
    def _():
        own_piece.wait()

    def piece_arrival(slot):
        return remote(lat_ref, pieces.at[slot], cs.at[0], cr.at[slot], sibling)

    for slot in range(4):

        @pl.when(jnp.logical_not((core == home) & (own_slot == slot)))
        def _(slot=slot):
            piece_arrival(slot).wait_recv()

    for half in (0, 1):
        a, b, _ = axes(half)
        lat[core * 2 + half, (a * 4 + b) * 2 + zl] = jnp.concatenate(
            [pieces[half * 2], pieces[half * 2 + 1]], axis=1
        )
        lat_copy(half, 0).start()
    for half in (0, 1):
        lat_copy(half, 0).wait_recv()
        lat_copy(half, 1).start()
        lat_copy(half, 2).start()
    out_first.start()
    out_local.start()
    for half in (0, 1):
        lat_copy(half, 1).wait_recv()
        lat_copy(half, 3).start()
        lat_copy(half, 2).wait_recv()
        lat_copy(half, 4).start()
    for half in (0, 1):
        lat_copy(half, 3).wait_recv()
        lat_copy(half, 4).wait_recv()
        lat_copy(half, 5).start()
        lat_copy(half, 6).start()
        sib_copy(half, 0).start()

    def small_wait(d, carry):
        w_copy(d)[1].wait()
        q_copy(d)[1].wait()
        return carry

    lax.fori_loop(1, ROWS, small_wait, 0)
    local_q.wait()
    local_w.wait()
    wkt[...] = wkv[...].reshape(512, 256)[:, :HEAD].T
    values[:, HEAD:] = jnp.ones((ROWS * TOK, HEAD), BF16)

    for half in (0, 1):
        lat_copy(half, 5).wait_recv()
        lat_copy(half, 7).start()
        lat_copy(half, 6).wait_recv()
        lat_copy(half, 8).start()
        sib_copy(half, 1).start()
        sib_copy(half, 2).start()
    out_first.wait_recv()
    out_local.wait()
    for half in (0, 1):
        lat_copy(half, 7).wait_recv()
        lat_copy(half, 8).wait_recv()
        sib_copy(half, 3).start()
        out_copy(half, 1).start()
        out_copy(half, 2).start()
    for half in (0, 1):
        for n in range(4):
            sib_copy(half, n).wait_recv()

    def project(r, carry):
        xx = lax.rem(r, 4)
        yy = lax.rem(r // 4, 4)
        zz = r // 16
        first = (xx * 4 + yy) * 2 + zz
        second = (yy * 4 + xx) * 2 + zz
        tokens = jnp.concatenate(
            [lat[0, first], lat[1, second], lat[2, first], lat[3, second]], axis=1
        )
        at = pl.multiple_of(r * TOK, TOK)
        keys_t[:, pl.ds(at, TOK)] = lax.dot_general(
            wkt[...], tokens, (((1,), (1,)), ((), ())), preferred_element_type=F32
        ).astype(BF16)
        values[pl.ds(at, TOK), :HEAD] = jnp.dot(
            tokens, wkv[...].reshape(512, 256)[:, HEAD:], preferred_element_type=F32
        ).astype(BF16)
        return carry

    lax.fori_loop(0, ROWS, project, 0)

    def att_copy(r, d):
        dst = feats.at[
            col,
            pl.ds(pl.multiple_of(row // 4 * STRIPE, STRIPE), STRIPE),
            pl.ds(pl.multiple_of(head_local * HEAD, HEAD), HEAD),
        ]
        return dst, remote(att.at[r], dst, hs.at[d], hr.at[d], (r, col))

    def out_steps(block):
        @pl.when(block == 2)
        def _():
            for half in (0, 1):
                out_copy(half, 1).wait_recv()
                out_copy(half, 3).start()
                out_copy(half, 2).wait_recv()
                out_copy(half, 4).start()

        @pl.when(block == 3)
        def _():
            for half in (0, 1):
                out_copy(half, 3).wait_recv()
                out_copy(half, 4).wait_recv()
                out_copy(half, 5).start()
                out_copy(half, 6).start()

        @pl.when(block == 7)
        def _():
            for half in (0, 1):
                out_copy(half, 5).wait_recv()
                out_copy(half, 7).start()
                out_copy(half, 6).wait_recv()
                out_copy(half, 8).start()

    def turn(query, first_key, allowed):
        first_key = pl.multiple_of(first_key, KB)
        scores = jnp.dot(query, keys_t[:, pl.ds(first_key, KB)], preferred_element_type=F32)
        if allowed is not None:
            scores = jnp.where(allowed, scores, NEG_FILL)
        before = top[:, :1]
        now = jnp.maximum(before, jnp.max(scores, axis=1, keepdims=True))
        weights = jnp.exp2((scores - now) * SCALE).astype(BF16)
        rescale = jnp.exp2((before - now) * SCALE)
        acc[...] = acc[...] * rescale + jnp.dot(
            weights, values[pl.ds(first_key, KB), :], preferred_element_type=F32
        )
        top[...] = jnp.broadcast_to(now, top.shape)

    def attend(block, carry):
        out_steps(block)
        query = queries[pl.ds(block * QROWS, QROWS)].reshape(QB, HEAD)
        acc[...] = jnp.zeros_like(acc)
        top[...] = jnp.full(top.shape, NEG_FILL, F32)

        def full(step, inner):
            turn(query, step * KB, None)
            return inner

        lax.fori_loop(0, block, full, 0)
        place = lax.broadcasted_iota(jnp.int32, (QB, KB), 0)
        key = lax.broadcasted_iota(jnp.int32, (QB, KB), 1)
        source = (
            (place >= STRIPE).astype(jnp.int32)
            + (place >= 2 * STRIPE).astype(jnp.int32)
            + (place >= 3 * STRIPE).astype(jnp.int32)
        )
        position = source * (TOK - STRIPE) + place + row // 4 * STRIPE
        turn(query, block * KB, key <= position)
        done = (acc[:, :HEAD] / acc[:, HEAD:]).astype(BF16)
        att[pl.ds(block * QROWS, QROWS)] = done.reshape(QROWS, STRIPE, HEAD)
        for j in range(QROWS):
            r = block * QROWS + j

            @pl.when(r != row)
            def _(r=r):
                att_copy(r, lax.rem(row - r + ROWS, ROWS))[1].start()

        return carry

    lax.fori_loop(0, BLOCKS, attend, 0)

    local_att = pltpu.make_async_copy(att.at[row], att_copy(row, 0)[0], ls.at[4])
    local_att.start()

    def att_wait(d, carry):
        att_copy(row, d)[1].wait_recv()
        return carry

    lax.fori_loop(1, ROWS, att_wait, 0)
    local_att.wait()

    def place_of(h, k):
        return h * 2 + k

    def feat_copy(n):
        if n == 0:
            src, to = feats.at[col], place_of(up(zh), core)
        elif n == 1:
            src, to = feats.at[col], place_of(down(zh), core)
        elif n == 2:
            src, to = feats.at[col], place_of(zh, 1 - core)
        elif n == 3:
            src, to = feats.at[place_of(down(zh), core), pl.ds(0, 192)], place_of(up(zh), core)
        elif n == 4:
            src, to = feats.at[place_of(up(zh), core), pl.ds(192, 192)], place_of(down(zh), core)
        elif n == 5:
            src, to = feats.at[place_of(down(zh), core)], place_of(zh, 1 - core)
        elif n == 6:
            src, to = feats.at[place_of(up(zh), core)], place_of(zh, 1 - core)
        else:
            src, to = feats.at[place_of(across(zh), core)], place_of(zh, 1 - core)
        return remote(src, src, zs.at[n], zr.at[n], (row, to))

    for n in range(3):
        feat_copy(n).start()
    for half in (0, 1):
        out_copy(half, 7).wait_recv()
        out_copy(half, 8).wait_recv()

    def mix(c, first):
        low = c // 4
        within = lax.rem(c, 4)
        weights = []
        for j in range(4):
            weights.append(wout[low, jnp.where(low == 0, j * 4 + within, within * 4 + j)])
        product = jnp.dot(
            feats[c], jnp.concatenate(weights, axis=0), preferred_element_type=F32
        )
        if first:
            total[...] = product
        else:
            total[...] += product

    mix(col, True)
    feat_copy(0).wait_recv()
    feat_copy(3).start()
    feat_copy(5).start()
    feat_copy(1).wait_recv()
    feat_copy(4).start()
    feat_copy(6).start()
    feat_copy(2).wait_recv()

    def mix_some(n, carry):
        h = jnp.where(n == 0, zh, jnp.where(lax.rem(n, 2) == 1, down(zh), up(zh)))
        k = jnp.where((n == 1) | (n == 2), core, 1 - core)
        mix(place_of(h, k), False)
        return carry

    lax.fori_loop(0, 3, mix_some, 0)
    feat_copy(3).wait_recv()
    feat_copy(4).wait_recv()
    feat_copy(7).start()
    feat_copy(5).wait_recv()
    feat_copy(6).wait_recv()
    lax.fori_loop(3, 5, mix_some, 0)
    mix(place_of(across(zh), core), False)
    feat_copy(7).wait_recv()
    mix(place_of(across(zh), 1 - core), False)
    out_ref[...] = total[...].astype(BF16)

    for d in (1, 2, 3):
        col_copy(d).wait_send()
    for half in (0, 1):
        for n in range(9):
            lat_copy(half, n).wait_send()
        for n in range(4):
            sib_copy(half, n).wait_send()
        for n in range(1, 9):
            out_copy(half, n).wait_send()
    out_first.wait_send()

    def att_sent(d, carry):
        att_copy(lax.rem(row - d + ROWS, ROWS), d)[1].wait_send()
        return carry

    lax.fori_loop(1, ROWS, att_sent, 0)
    for n in range(8):
        feat_copy(n).wait_send()


def per_device(latent, w_kv, queries, w_out):
    dma = pltpu.SemaphoreType.DMA
    vmem = pltpu.VMEM
    return pl.pallas_call(
        kernel,
        out_shape=jax.ShapeDtypeStruct((TOK, w_out.shape[1]), BF16),
        in_specs=[pl.BlockSpec(memory_space=pltpu.VMEM)] * 4,
        out_specs=pl.BlockSpec(memory_space=pltpu.VMEM),
        scratch_shapes=[
            vmem((4, TOK, 64), BF16),
            vmem((4, ROWS, TOK, 128), BF16),
            vmem((ROWS, 16, 256), BF16),
            vmem((128, 512), BF16),
            vmem((ROWS, STRIPE, HEAD), BF16),
            vmem((HEAD, ROWS * TOK), BF16),
            vmem((ROWS * TOK, 256), BF16),
            vmem((ROWS, STRIPE, HEAD), BF16),
            vmem((8, TOK, 512), BF16),
            vmem((2, 16, 128, 896), BF16),
            vmem((QB, 256), F32),
            vmem((QB, 128), F32),
            vmem((TOK, 896), F32),
            dma((4,)), dma((4,)),
            dma((ROWS,)), dma((ROWS,)),
            dma((ROWS,)), dma((ROWS,)),
            dma((2, 9)), dma((2, 9)),
            dma((2, 4)), dma((2, 4)),
            dma((2, 9)), dma((2, 9)),
            dma((ROWS,)), dma((ROWS,)),
            dma((8,)), dma((8,)),
            dma((5,)),
        ],
        compiler_params=pltpu.CompilerParams(
            collective_id=0, has_side_effects=True, vmem_limit_bytes=60 * 1024 * 1024
        ),
        cost_estimate=pl.CostEstimate(
            flops=12_000_000_000, bytes_accessed=2_000_000, transcendentals=11_000_000
        ),
    )(latent, w_kv, queries, w_out)


def solution(mesh):
    spec = P("row", "col")
    return jax.shard_map(
        per_device, mesh=mesh, in_specs=(spec,) * 4, out_specs=spec, check_vma=False
    )
```

```python
import functools

import jax
import jax.numpy as jnp
from jax import lax
from jax.experimental import pallas as pl
from jax.experimental.pallas import tpu as pltpu
from jax.sharding import PartitionSpec as P

HEAD = 128
NEG_FILL = -1e30
MESH = pl.DeviceIdType.MESH
BF16 = jnp.bfloat16
F32 = jnp.float32

ROWS = 32
TOK = 384
STRIPE = 48
QROWS = 8
DIAG = 4
QB = QROWS * STRIPE
KB = QROWS * TOK
BLOCKS = ROWS // QROWS
SCALE = HEAD**-0.5 * 1.4426950408889634


def kernel(
    lat_ref, wkv_ref, q_ref, wout_ref, out_ref,
    lat, wkv, wkt, queries, keys_t, values, att, feats, wout, acc, top, total,
    cs, cr, qs, qr, ws, wr, gs, gr, ss, sr, os, orr, hs, hr, zs, zr, ls,
):
    row = lax.axis_index("row")
    col = lax.axis_index("col")
    x = lax.rem(row, 4)
    y = lax.rem(row // 4, 4)
    zl = row // 16
    zh = col // 2
    core = lax.rem(col, 2)
    sibling = (row, zh * 2 + 1 - core)

    def row_of(xx, yy, zz):
        return zz * 16 + yy * 4 + xx

    def up(v):
        return lax.rem(v + 1, 4)

    def down(v):
        return lax.rem(v + 3, 4)

    def across(v):
        return lax.rem(v + 2, 4)

    def remote(src, dst, send, recv, device):
        return pltpu.make_async_remote_copy(
            src_ref=src, dst_ref=dst, send_sem=send, recv_sem=recv,
            device_id=device, device_id_type=MESH,
        )

    barrier = pltpu.get_barrier_semaphore()

    def greet_row(d, carry):
        pl.semaphore_signal(
            barrier, inc=1, device_id=(lax.rem(row + d, ROWS), col), device_id_type=MESH
        )
        return carry

    def greet_col(d, carry):
        pl.semaphore_signal(
            barrier, inc=1, device_id=(row, lax.rem(col + d, 8)), device_id_type=MESH
        )
        return carry

    lax.fori_loop(1, 8, greet_col, 0)
    lax.fori_loop(1, ROWS, greet_row, 0)
    pl.semaphore_wait(barrier, ROWS - 1 + 7)

    home = zh // 2
    own_slot = lax.rem(zh, 2) * 2 + core
    slots = ((x * 4 + y) * 2 + zl, (y * 4 + x) * 2 + zl)
    own_place = lat.at[
        zh,
        jnp.where(lax.rem(zh, 2) == 0, slots[0], slots[1]),
        pl.ds(pl.multiple_of(core * 64, 64), 64),
    ]

    def col_copy(d):
        dst = (row, lax.rem(zh + d, 4) * 2 + home)
        return remote(lat_ref, own_place, cs.at[d], cr.at[own_slot], dst)

    for d in (2, 1, 3):
        col_copy(d).start()

    @pl.when(core != home)
    def _():
        col_copy(0).start()

    own_piece = pltpu.make_async_copy(lat_ref, own_place, ls.at[0])

    @pl.when(core == home)
    def _():
        own_piece.start()

    head_local = x

    def q_part(peer):
        return q_ref.at[
            pl.ds(pl.multiple_of(peer // 4 * STRIPE, STRIPE), STRIPE),
            pl.ds(pl.multiple_of(lax.rem(peer, 4) * HEAD, HEAD), HEAD),
        ]

    def w_part(peer):
        return wkv_ref.at[:, pl.ds(pl.multiple_of(lax.rem(peer, 4) * 256, 256), 256)]

    def q_copy(d):
        peer = lax.rem(row + d, ROWS)
        return remote(q_part(peer), queries.at[row], qs.at[d], qr.at[d], (peer, col))

    def w_copy(d):
        peer = lax.rem(row + d, ROWS)
        return remote(w_part(peer), wkv.at[row], ws.at[d], wr.at[d], (peer, col))

    def small_start(d, carry):
        w_copy(d).start()
        q_copy(d).start()
        return carry

    def axes(half):
        if half == 0:
            return x, y, lambda aa, bb, zz: row_of(aa, bb, zz)
        return y, x, lambda aa, bb, zz: row_of(bb, aa, zz)

    def lat_copy(half, n):
        a, b, dev = axes(half)
        buf = lat.at[core * 2 + half]
        across_b = (b, down(b), up(b), across(b))

        def at(aa, bb, zz, count):
            return buf.at[pl.ds((aa * 4 + bb) * 2 + zz, count)]

        if n == 0:
            src, to = at(a, b, zl, 1), dev(a, b, 1 - zl)
        elif n <= 4:
            src = at(a, b, zl if n <= 2 else 1 - zl, 1)
            to = dev(a, up(b) if n % 2 == 1 else down(b), zl)
        elif n == 5:
            src, to = at(a, down(b), zl, 1), dev(a, up(b), zl)
        elif n == 6:
            src, to = at(a, up(b), 1 - zl, 1), dev(a, down(b), zl)
        elif n < 11:
            src, to = at(a, across_b[n - 7], 0, 2), dev(up(a), b, zl)
        elif n < 15:
            src, to = at(a, across_b[n - 11], 0, 2), dev(down(a), b, zl)
        elif n < 19:
            src, to = at(down(a), across_b[n - 15], 0, 1), dev(up(a), b, zl)
        else:
            src, to = at(up(a), across_b[n - 19], 1, 1), dev(down(a), b, zl)
        return remote(src, src, gs.at[half, n], gr.at[half, n], (to, col))

    def sib_copy(half, g, j):
        a, b, _ = axes(half)
        aa = (a, down(a), up(a), across(a))[g]
        bb = (b, down(b), up(b), across(b))[j]
        src = lat.at[core * 2 + half, pl.ds((aa * 4 + bb) * 2, 2)]
        return remote(src, src, ss.at[half, g * 4 + j], sr.at[half, g * 4 + j], sibling)

    def out_copy(half, n):
        a, b, dev = axes(half)
        buf = wout.at[half]
        across_b = (b, down(b), up(b), across(b))
        if n <= 2:
            src = buf.at[a * 4 + b]
            to = dev(a, up(b) if n == 1 else down(b), zl)
        elif n == 3:
            src, to = buf.at[a * 4 + down(b), pl.ds(0, 64)], dev(a, up(b), zl)
        elif n == 4:
            src, to = buf.at[a * 4 + up(b), pl.ds(64, 64)], dev(a, down(b), zl)
        elif n < 9:
            src, to = buf.at[a * 4 + across_b[n - 5]], dev(up(a), b, zl)
        elif n < 13:
            src, to = buf.at[a * 4 + across_b[n - 9]], dev(down(a), b, zl)
        elif n < 17:
            src, to = buf.at[down(a) * 4 + across_b[n - 13], pl.ds(0, 64)], dev(up(a), b, zl)
        else:
            src, to = buf.at[up(a) * 4 + across_b[n - 17], pl.ds(64, 64)], dev(down(a), b, zl)
        return remote(src, src, os.at[half, n], orr.at[half, n], (to, col))

    own_out = wout.at[zl, jnp.where(zl == 0, x * 4 + y, y * 4 + x)]
    out_first = remote(wout_ref, own_out, os.at[0, 0], orr.at[0, 0], (row_of(x, y, 1 - zl), col))
    out_local = pltpu.make_async_copy(wout_ref, own_out, ls.at[3])

    out_local.start()
    out_local.wait()
    for half in (0, 1):

        @pl.when(zl == half)
        def _(half=half):
            for n in (1, 2, 5, 9):
                out_copy(half, n).start()

    @pl.when(core != home)
    def _():
        col_copy(0).wait_send()

    @pl.when(core == home)
    def _():
        own_piece.wait()

    def piece_arrival(slot):
        return remote(lat_ref, own_place, cs.at[0], cr.at[slot], sibling)

    for slot in range(4):

        @pl.when(jnp.logical_not((core == home) & (own_slot == slot)))
        def _(slot=slot):
            piece_arrival(slot).wait_recv()

    for half in (0, 1):
        for n in (0, 1, 2):
            lat_copy(half, n).start()
    lax.fori_loop(1, ROWS, small_start, 0)
    local_q = pltpu.make_async_copy(q_part(row), queries.at[row], ls.at[1])
    local_w = pltpu.make_async_copy(w_part(row), wkv.at[row], ls.at[2])
    local_q.start()
    local_w.start()
    for half in (0, 1):
        lat_copy(half, 0).wait_recv()
        for n in (3, 4, 7, 11):
            lat_copy(half, n).start()
        sib_copy(half, 0, 0).start()
    out_first.start()
    for half in (0, 1):
        lat_copy(half, 1).wait_recv()
        lat_copy(half, 5).start()
        lat_copy(half, 4).wait_recv()
        lat_copy(half, 6).start()
    for half in (0, 1):
        lat_copy(half, 3).wait_recv()
        for n in (8, 12):
            lat_copy(half, n).start()
        sib_copy(half, 0, 1).start()
        lat_copy(half, 2).wait_recv()
        for n in (9, 13):
            lat_copy(half, n).start()
        sib_copy(half, 0, 2).start()
    for half in (0, 1):
        lat_copy(half, 5).wait_recv()
        lat_copy(half, 6).wait_recv()
        for n in (10, 14):
            lat_copy(half, n).start()
        sib_copy(half, 0, 3).start()

    def small_wait(d, carry):
        w_copy(d).wait()
        q_copy(d).wait()
        return carry

    lax.fori_loop(1, ROWS, small_wait, 0)
    local_q.wait()
    local_w.wait()
    wkt[...] = wkv[...].reshape(512, 256).T
    values[:, HEAD:] = jnp.ones((ROWS * TOK, HEAD), BF16)

    for j in range(4):
        for half in (0, 1):
            lat_copy(half, 7 + j).wait_recv()
            lat_copy(half, 15 + j).start()
            sib_copy(half, 1, j).start()
            lat_copy(half, 11 + j).wait_recv()
            lat_copy(half, 19 + j).start()
            sib_copy(half, 2, j).start()
    for half in (0, 1):
        for g in range(3):
            for j in range(4):
                sib_copy(half, g, j).wait_recv()

    def project(i, carry):
        later = i - 9
        xx = jnp.where(i < 9, x + lax.rem(i, 3) + 3, jnp.where(later < 4, x + 2, x + later - 1))
        yy = jnp.where(i < 9, y + i // 3 + 3, jnp.where(later < 4, y + later, y + 2))
        xx = lax.rem(xx, 4)
        yy = lax.rem(yy, 4)
        for zz in (0, 1):
            first = (xx * 4 + yy) * 2 + zz
            second = (yy * 4 + xx) * 2 + zz
            tokens = jnp.concatenate(
                [lat[0, first], lat[1, second], lat[2, first], lat[3, second]], axis=0
            )
            at = pl.multiple_of(row_of(xx, yy, zz) * TOK, TOK)
            pair = jnp.dot(wkt[...], tokens, preferred_element_type=F32)
            keys_t[:, pl.ds(at, TOK)] = pair[:HEAD].astype(BF16)
            values[pl.ds(at, TOK), :HEAD] = pair[HEAD:].T.astype(BF16)
        return carry

    def last_group(j):
        for half in (0, 1):
            lat_copy(half, 15 + j).wait_recv()
            lat_copy(half, 19 + j).wait_recv()
            sib_copy(half, 3, j).start()

    lax.fori_loop(0, 3, project, 0)
    last_group(0)
    lax.fori_loop(3, 6, project, 0)
    last_group(1)
    out_first.wait_recv()
    for half in (0, 1):
        @pl.when(zl != half)
        def _(half=half):
            for n in (1, 2, 5, 9):
                out_copy(half, n).start()
    lax.fori_loop(6, 9, project, 0)
    last_group(2)
    last_group(3)
    for half in (0, 1):
        for j in range(4):
            sib_copy(half, 3, j).wait_recv()
    lax.fori_loop(9, 16, project, 0)

    att_place = feats.at[
        col,
        pl.ds(pl.multiple_of(row // 4 * STRIPE, STRIPE), STRIPE),
        pl.ds(pl.multiple_of(head_local * HEAD, HEAD), HEAD),
    ]

    def att_copy(r, d):
        return remote(att.at[r], att_place, hs.at[d], hr.at[d], (r, col))

    local_att = pltpu.make_async_copy(att.at[row], att_place, ls.at[4])

    def place_of(h, k):
        return h * 2 + k

    def feat_copy(n, part):
        lanes = pl.ds(pl.multiple_of(part * 256, 256), 256)

        def at(place, first, count):
            return feats.at[place, pl.ds(first, count), lanes]

        if n == 0:
            src, to = at(col, 0, TOK), place_of(up(zh), core)
        elif n == 1:
            src, to = at(col, 0, TOK), place_of(down(zh), core)
        elif n == 2:
            src, to = at(col, 0, TOK), place_of(zh, 1 - core)
        elif n == 3:
            src, to = at(place_of(down(zh), core), 0, 192), place_of(up(zh), core)
        elif n == 4:
            src, to = at(place_of(up(zh), core), 192, 192), place_of(down(zh), core)
        elif n == 5:
            src, to = at(place_of(down(zh), core), 0, TOK), place_of(zh, 1 - core)
        elif n == 6:
            src, to = at(place_of(up(zh), core), 0, TOK), place_of(zh, 1 - core)
        else:
            src, to = at(place_of(across(zh), core), 0, TOK), place_of(zh, 1 - core)
        return remote(src, src, zs.at[part, n], zr.at[part, n], (row, to))

    def feat_start(part):
        @pl.when(head_local // 2 == part)
        def _():
            local_att.start()

        def arrival(j, carry):
            source = j // 2 * 4 + part * 2 + lax.rem(j, 2)

            @pl.when(source != row)
            def _():
                att_copy(row, lax.rem(source - row + ROWS, ROWS)).wait_recv()

            return carry

        lax.fori_loop(0, ROWS // 2, arrival, 0)

        @pl.when(head_local // 2 == part)
        def _():
            local_att.wait()

        for n in range(3):
            feat_copy(n, part).start()

    def feat_forward(part):
        feat_copy(0, part).wait_recv()
        feat_copy(3, part).start()
        feat_copy(5, part).start()
        feat_copy(1, part).wait_recv()
        feat_copy(4, part).start()
        feat_copy(6, part).start()

    def feat_hand_over(part):
        feat_copy(3, part).wait_recv()
        feat_copy(4, part).wait_recv()
        feat_copy(7, part).start()

    turned = head_local // 2
    my_block = row // QROWS
    early = jnp.where(my_block == 3, 1, 0)

    def beside(tick):
        @pl.when(tick == 0)
        def _():
            for half in (0, 1):
                out_copy(half, 1).wait_recv()
                for n in (3, 6, 10):
                    out_copy(half, n).start()
                out_copy(half, 2).wait_recv()
                for n in (4, 7, 11):
                    out_copy(half, n).start()

        @pl.when(tick == 1)
        def _():
            for half in (0, 1):
                for n in (3, 4):
                    out_copy(half, n).wait_recv()
                for n in (8, 12):
                    out_copy(half, n).start()
                out_copy(half, 5).wait_recv()
                out_copy(half, 13).start()
                out_copy(half, 9).wait_recv()
                out_copy(half, 17).start()

        @pl.when(
            ((tick == 2) & (my_block == 0))
            | ((tick == 3) & (my_block == 1))
            | ((tick == 4) & (my_block == 3))
            | ((tick == 5) & (my_block == 2))
        )
        def _():
            feat_start(early)

        @pl.when(((tick == 4) & (my_block == 0)) | ((tick == 5) & (my_block == 1)))
        def _():
            feat_start(1 - early)

        @pl.when(tick == 3)
        def _():
            for half in (0, 1):
                out_copy(half, 6).wait_recv()
                out_copy(half, 14).start()
                out_copy(half, 10).wait_recv()
                out_copy(half, 18).start()

        @pl.when(tick == 5)
        def _():
            for half in (0, 1):
                out_copy(half, 7).wait_recv()
                out_copy(half, 15).start()
                out_copy(half, 11).wait_recv()
                out_copy(half, 19).start()

    def turn(query, start, first_key, keys, allowed):
        scores = jnp.dot(
            query[start:], keys_t[:, pl.ds(first_key, keys)], preferred_element_type=F32
        )
        if allowed is not None:
            scores = jnp.where(allowed, scores, NEG_FILL)
        before = top[start:, :1]
        now = jnp.maximum(before, jnp.max(scores, axis=1, keepdims=True))
        weights = jnp.exp2((scores - now) * SCALE).astype(BF16)
        rescale = jnp.exp2((before - now) * SCALE)
        acc[start:, :] = acc[start:, :] * rescale + jnp.dot(
            weights, values[pl.ds(first_key, keys), :], preferred_element_type=F32
        )
        top[start:, :] = jnp.broadcast_to(now, (QB - start, HEAD))

    def attend(turn_index, carry):
        block = lax.rem(turn_index + 3 * turned, BLOCKS)
        before = jnp.where(
            turned == 0,
            turn_index * (turn_index - 1) // 2,
            jnp.where(turn_index >= 2, turn_index + 1, 0),
        )
        query = queries[pl.ds(block * QROWS, QROWS)].reshape(QB, HEAD)
        acc[...] = jnp.zeros_like(acc)
        top[...] = jnp.full(top.shape, NEG_FILL, F32)

        def full(step, inner):
            beside(before + step)
            turn(query, 0, pl.multiple_of(step * KB, KB), KB, None)
            return inner

        lax.fori_loop(0, block, full, 0)
        for part in range(QROWS // DIAG):
            start = part * DIAG * STRIPE
            shape = (QB - start, DIAG * TOK)
            place = lax.broadcasted_iota(jnp.int32, shape, 0)
            key = lax.broadcasted_iota(jnp.int32, shape, 1)
            source = sum(
                (place >= STRIPE * j).astype(jnp.int32) for j in range(1, QROWS - part * DIAG)
            )
            position = source * (TOK - STRIPE) + place + row // 4 * STRIPE
            first_key = pl.multiple_of(block * KB + part * DIAG * TOK, DIAG * TOK)
            turn(query, start, first_key, DIAG * TOK, key <= position)
        done = (acc[:, :HEAD] / acc[:, HEAD:]).astype(BF16)
        att[pl.ds(block * QROWS, QROWS)] = done.reshape(QROWS, STRIPE, HEAD)
        for j in range(QROWS):
            r = block * QROWS + j

            @pl.when(r != row)
            def _(r=r):
                att_copy(r, lax.rem(row - r + ROWS, ROWS)).start()

        return carry

    lax.fori_loop(0, BLOCKS, attend, 0)

    for half in (0, 1):
        out_copy(half, 8).wait_recv()
        out_copy(half, 16).start()
        out_copy(half, 12).wait_recv()
        out_copy(half, 20).start()

    @pl.when(my_block >= 2)
    def _():
        feat_start(1 - early)

    feat_forward(early)

    feat_forward(1 - early)
    feat_hand_over(early)
    for half in (0, 1):
        for n in range(13, 21):
            out_copy(half, n).wait_recv()

    def mix(c, part, first=False):
        low = c // 4
        within = lax.rem(c, 4)
        weights = []
        for j in (0, 1):
            xx = part * 2 + j
            weights.append(wout[low, jnp.where(low == 0, xx * 4 + within, within * 4 + xx)])
        heads = feats[c, :, pl.ds(pl.multiple_of(part * 256, 256), 256)]
        product = jnp.dot(heads, jnp.concatenate(weights, axis=0), preferred_element_type=F32)
        if first:
            total[...] = product
        else:
            total[...] += product

    def mix_some(n, part):
        h = jnp.where(n == 0, zh, jnp.where(lax.rem(n, 2) == 1, down(zh), up(zh)))
        k = jnp.where((n == 1) | (n == 2), core, 1 - core)
        mix(place_of(h, k), part)
        return part

    mix(col, early, True)
    for part in (early, 1 - early):
        if part is not early:
            mix(col, part)
        feat_copy(2, part).wait_recv()
        lax.fori_loop(0, 3, mix_some, part)
        feat_copy(5, part).wait_recv()
        feat_copy(6, part).wait_recv()
        lax.fori_loop(3, 5, mix_some, part)
        if part is not early:
            feat_hand_over(part)
        mix(place_of(across(zh), core), part)
        feat_copy(7, part).wait_recv()
        mix(place_of(across(zh), 1 - core), part)
    out_ref[...] = total[...].astype(BF16)

    for d in (1, 2, 3):
        col_copy(d).wait_send()
    for half in (0, 1):
        for n in range(23):
            lat_copy(half, n).wait_send()
        for g in range(4):
            for j in range(4):
                sib_copy(half, g, j).wait_send()
        for n in range(1, 21):
            out_copy(half, n).wait_send()
    out_first.wait_send()

    def att_sent(d, carry):
        att_copy(lax.rem(row - d + ROWS, ROWS), d).wait_send()
        return carry

    lax.fori_loop(1, ROWS, att_sent, 0)
    for part in (0, 1):
        for n in range(8):
            feat_copy(n, part).wait_send()


def per_device(latent, w_kv, queries, w_out):
    dma = pltpu.SemaphoreType.DMA
    vmem = pltpu.VMEM
    return pl.pallas_call(
        kernel,
        out_shape=jax.ShapeDtypeStruct((TOK, w_out.shape[1]), BF16),
        in_specs=[pl.BlockSpec(memory_space=pltpu.VMEM)] * 4,
        out_specs=pl.BlockSpec(memory_space=pltpu.VMEM),
        scratch_shapes=[
            vmem((4, ROWS, 128, TOK), BF16),
            vmem((ROWS, 16, 256), BF16),
            vmem((256, 512), BF16),
            vmem((ROWS, STRIPE, HEAD), BF16),
            vmem((HEAD, ROWS * TOK), BF16),
            vmem((ROWS * TOK, 256), BF16),
            vmem((ROWS, STRIPE, HEAD), BF16),
            vmem((8, TOK, 512), BF16),
            vmem((2, 16, 128, 896), BF16),
            vmem((QB, 256), F32),
            vmem((QB, 128), F32),
            vmem((TOK, 896), F32),
            dma((4,)), dma((4,)),
            dma((ROWS,)), dma((ROWS,)),
            dma((ROWS,)), dma((ROWS,)),
            dma((2, 23)), dma((2, 23)),
            dma((2, 16)), dma((2, 16)),
            dma((2, 21)), dma((2, 21)),
            dma((ROWS,)), dma((ROWS,)),
            dma((2, 8)), dma((2, 8)),
            dma((5,)),
        ],
        compiler_params=pltpu.CompilerParams(
            collective_id=0, has_side_effects=True, vmem_limit_bytes=60 * 1024 * 1024
        ),
        cost_estimate=pl.CostEstimate(
            flops=12_000_000_000, bytes_accessed=2_000_000, transcendentals=11_000_000
        ),
    )(latent.T, w_kv, queries, w_out)


def solution(mesh):
    spec = P("row", "col")
    return jax.shard_map(
        per_device, mesh=mesh, in_specs=(spec,) * 4, out_specs=spec, check_vma=False
    )
```

```python
import functools

import jax
import jax.numpy as jnp
from jax import lax
from jax.experimental import pallas as pl
from jax.experimental.pallas import tpu as pltpu
from jax.sharding import PartitionSpec as P

HEAD = 128
NEG_FILL = -1e30
MESH = pl.DeviceIdType.MESH
BF16 = jnp.bfloat16
F32 = jnp.float32

ROWS = 32
TOK = 384
STRIPE = 48
QROWS = 8
DIAG = 4
QB = QROWS * STRIPE
KB = QROWS * TOK
BLOCKS = ROWS // QROWS
SCALE = HEAD**-0.5 * 1.4426950408889634


def kernel(
    lat_ref, wkv_ref, q_ref, wout_ref, out_ref,
    lat, wkv, wkt, queries, keys_t, values, att, feats, wout, acc, top, total,
    cs, cr, qs, qr, ws, wr, gs, gr, ss, sr, os, orr, hs, hr, zs, zr, ls,
):
    row = lax.axis_index("row")
    col = lax.axis_index("col")
    x = lax.rem(row, 4)
    y = lax.rem(row // 4, 4)
    zl = row // 16
    zh = col // 2
    core = lax.rem(col, 2)
    sibling = (row, zh * 2 + 1 - core)

    def row_of(xx, yy, zz):
        return zz * 16 + yy * 4 + xx

    def up(v):
        return lax.rem(v + 1, 4)

    def down(v):
        return lax.rem(v + 3, 4)

    def across(v):
        return lax.rem(v + 2, 4)

    def remote(src, dst, send, recv, device):
        return pltpu.make_async_remote_copy(
            src_ref=src, dst_ref=dst, send_sem=send, recv_sem=recv,
            device_id=device, device_id_type=MESH,
        )

    barrier = pltpu.get_barrier_semaphore()

    def greet_row(d, carry):
        pl.semaphore_signal(
            barrier, inc=1, device_id=(lax.rem(row + d, ROWS), col), device_id_type=MESH
        )
        return carry

    def greet_col(d, carry):
        pl.semaphore_signal(
            barrier, inc=1, device_id=(row, lax.rem(col + d, 8)), device_id_type=MESH
        )
        return carry

    lax.fori_loop(1, 8, greet_col, 0)
    lax.fori_loop(1, ROWS, greet_row, 0)
    pl.semaphore_wait(barrier, ROWS - 1 + 7)

    home = zh // 2
    own_slot = lax.rem(zh, 2) * 2 + core
    slots = ((x * 4 + y) * 2 + zl, (y * 4 + x) * 2 + zl)
    own_place = lat.at[
        zh,
        jnp.where(lax.rem(zh, 2) == 0, slots[0], slots[1]),
        pl.ds(pl.multiple_of(core * 64, 64), 64),
    ]

    def col_copy(d):
        dst = (row, lax.rem(zh + d, 4) * 2 + home)
        return remote(lat_ref, own_place, cs.at[d], cr.at[own_slot], dst)

    for d in (2, 1, 3):
        col_copy(d).start()

    @pl.when(core != home)
    def _():
        col_copy(0).start()

    own_piece = pltpu.make_async_copy(lat_ref, own_place, ls.at[0])

    @pl.when(core == home)
    def _():
        own_piece.start()

    head_local = x

    def q_part(peer):
        return q_ref.at[
            pl.ds(pl.multiple_of(peer // 4 * STRIPE, STRIPE), STRIPE),
            pl.ds(pl.multiple_of(lax.rem(peer, 4) * HEAD, HEAD), HEAD),
        ]

    def w_part(peer):
        return wkv_ref.at[:, pl.ds(pl.multiple_of(lax.rem(peer, 4) * 256, 256), 256)]

    def q_copy(d):
        peer = lax.rem(row + d, ROWS)
        return remote(q_part(peer), queries.at[row], qs.at[d], qr.at[d], (peer, col))

    def w_copy(d):
        peer = lax.rem(row + d, ROWS)
        return remote(w_part(peer), wkv.at[row], ws.at[d], wr.at[d], (peer, col))

    def small_start(d, carry):
        w_copy(d).start()
        q_copy(d).start()
        return carry

    def axes(half):
        if half == 0:
            return x, y, lambda aa, bb, zz: row_of(aa, bb, zz)
        return y, x, lambda aa, bb, zz: row_of(bb, aa, zz)

    def lat_copy(half, n):
        a, b, dev = axes(half)
        buf = lat.at[core * 2 + half]
        across_b = (b, down(b), up(b), across(b))

        def at(aa, bb, zz, count):
            return buf.at[pl.ds((aa * 4 + bb) * 2 + zz, count)]

        if n == 0:
            src, to = at(a, b, zl, 1), dev(a, b, 1 - zl)
        elif n <= 4:
            src = at(a, b, zl if n <= 2 else 1 - zl, 1)
            to = dev(a, up(b) if n % 2 == 1 else down(b), zl)
        elif n == 5:
            src, to = at(a, down(b), zl, 1), dev(a, up(b), zl)
        elif n == 6:
            src, to = at(a, up(b), 1 - zl, 1), dev(a, down(b), zl)
        elif n < 11:
            src, to = at(a, across_b[n - 7], 0, 2), dev(up(a), b, zl)
        elif n < 15:
            src, to = at(a, across_b[n - 11], 0, 2), dev(down(a), b, zl)
        elif n < 19:
            src, to = at(down(a), across_b[n - 15], 0, 1), dev(up(a), b, zl)
        else:
            src, to = at(up(a), across_b[n - 19], 1, 1), dev(down(a), b, zl)
        return remote(src, src, gs.at[half, n], gr.at[half, n], (to, col))

    def sib_copy(half, g, j):
        a, b, _ = axes(half)
        aa = (a, down(a), up(a), across(a))[g]
        bb = (b, down(b), up(b), across(b))[j]
        src = lat.at[core * 2 + half, pl.ds((aa * 4 + bb) * 2, 2)]
        return remote(src, src, ss.at[half, g * 4 + j], sr.at[half, g * 4 + j], sibling)

    def out_copy(half, n):
        a, b, dev = axes(half)
        buf = wout.at[half]
        across_b = (b, down(b), up(b), across(b))
        if n <= 2:
            src = buf.at[a * 4 + b]
            to = dev(a, up(b) if n == 1 else down(b), zl)
        elif n == 3:
            src, to = buf.at[a * 4 + down(b), pl.ds(0, 64)], dev(a, up(b), zl)
        elif n == 4:
            src, to = buf.at[a * 4 + up(b), pl.ds(64, 64)], dev(a, down(b), zl)
        elif n < 9:
            src, to = buf.at[a * 4 + across_b[n - 5]], dev(up(a), b, zl)
        elif n < 13:
            src, to = buf.at[a * 4 + across_b[n - 9]], dev(down(a), b, zl)
        elif n < 17:
            src, to = buf.at[down(a) * 4 + across_b[n - 13], pl.ds(0, 64)], dev(up(a), b, zl)
        else:
            src, to = buf.at[up(a) * 4 + across_b[n - 17], pl.ds(64, 64)], dev(down(a), b, zl)
        return remote(src, src, os.at[half, n], orr.at[half, n], (to, col))

    def out_step(half, landed, sent):
        for n in landed:
            out_copy(half, n).wait_recv()
        for n in sent:
            out_copy(half, n).start()

    first_steps = {
        0: [((1,), (3, 6, 10)), ((2,), (4, 7, 11)), ((5,), (13,)), ((9,), (17,))],
        1: [((3, 4), (8, 12)), ((6,), (14,)), ((10,), (18,))],
        2: [((7,), (15,)), ((11,), (19,))],
        3: [((8,), (16,)), ((12,), (20,))],
    }
    second_steps = {
        0: [((), (1, 2, 5, 9))],
        1: [((1,), (3, 6, 10)), ((2,), (4, 7, 11))],
        2: [((5,), (13,)), ((9,), (17,))],
        3: [((3, 4), (8, 12)), ((6,), (14,)), ((10,), (18,))],
        4: [((7,), (15,)), ((11,), (19,))],
        5: [((8,), (16,)), ((12,), (20,))],
    }

    def out_stage(stage):
        if stage == 0:
            out_first.wait_recv()
        for steps, own in ((second_steps, False), (first_steps, True)):
            for half in (0, 1):

                @pl.when((zl == half) if own else (zl != half))
                def _(half=half, steps=steps):
                    for landed, sent in steps.get(stage, []):
                        out_step(half, landed, sent)

    own_out = wout.at[zl, jnp.where(zl == 0, x * 4 + y, y * 4 + x)]
    out_first = remote(wout_ref, own_out, os.at[0, 0], orr.at[0, 0], (row_of(x, y, 1 - zl), col))
    out_local = pltpu.make_async_copy(wout_ref, own_out, ls.at[3])

    lax.fori_loop(1, ROWS, small_start, 0)
    local_q = pltpu.make_async_copy(q_part(row), queries.at[row], ls.at[1])
    local_w = pltpu.make_async_copy(w_part(row), wkv.at[row], ls.at[2])
    local_q.start()
    local_w.start()
    out_local.start()
    out_local.wait()
    for half in (0, 1):

        @pl.when(zl == half)
        def _(half=half):
            for n in (1, 2, 5, 9):
                out_copy(half, n).start()

    @pl.when(core != home)
    def _():
        col_copy(0).wait_send()

    @pl.when(core == home)
    def _():
        own_piece.wait()

    def piece_arrival(slot):
        return remote(lat_ref, own_place, cs.at[0], cr.at[slot], sibling)

    for slot in range(4):

        @pl.when(jnp.logical_not((core == home) & (own_slot == slot)))
        def _(slot=slot):
            piece_arrival(slot).wait_recv()

    for half in (0, 1):
        for n in (0, 1, 2):
            lat_copy(half, n).start()
    for half in (0, 1):
        lat_copy(half, 0).wait_recv()
        for n in (3, 4, 7, 11):
            lat_copy(half, n).start()
        sib_copy(half, 0, 0).start()
    out_first.start()
    for half in (0, 1):
        lat_copy(half, 1).wait_recv()
        lat_copy(half, 5).start()
        lat_copy(half, 4).wait_recv()
        lat_copy(half, 6).start()
    for half in (0, 1):
        lat_copy(half, 3).wait_recv()
        for n in (8, 12):
            lat_copy(half, n).start()
        sib_copy(half, 0, 1).start()
        lat_copy(half, 2).wait_recv()
        for n in (9, 13):
            lat_copy(half, n).start()
        sib_copy(half, 0, 2).start()
    for half in (0, 1):
        lat_copy(half, 5).wait_recv()
        lat_copy(half, 6).wait_recv()
        for n in (10, 14):
            lat_copy(half, n).start()
        sib_copy(half, 0, 3).start()

    def small_wait(d, carry):
        w_copy(d).wait()
        q_copy(d).wait()
        return carry

    lax.fori_loop(1, ROWS, small_wait, 0)
    local_q.wait()
    local_w.wait()
    wkt[...] = wkv[...].reshape(512, 256).T
    values[:, HEAD:] = jnp.ones((ROWS * TOK, HEAD), BF16)

    for j in range(4):
        for half in (0, 1):
            lat_copy(half, 7 + j).wait_recv()
            lat_copy(half, 15 + j).start()
            sib_copy(half, 1, j).start()
            lat_copy(half, 11 + j).wait_recv()
            lat_copy(half, 19 + j).start()
            sib_copy(half, 2, j).start()
    for half in (0, 1):
        for g in range(3):
            for j in range(4):
                sib_copy(half, g, j).wait_recv()

    def project(i, carry):
        later = i - 9
        j = later // 2
        beyond = jnp.where(j == 0, 0, jnp.where(j == 1, 3, jnp.where(j == 2, 1, 2)))
        even = lax.rem(later + 10, 2) == 0
        xx = jnp.where(i < 9, x + lax.rem(i, 3) + 3, jnp.where(even, x + 2, x + beyond))
        yy = jnp.where(i < 9, y + i // 3 + 3, jnp.where(even, y + beyond, y + 2))
        xx = lax.rem(xx, 4)
        yy = lax.rem(yy, 4)
        for zz in (0, 1):
            first = (xx * 4 + yy) * 2 + zz
            second = (yy * 4 + xx) * 2 + zz
            tokens = jnp.concatenate(
                [lat[0, first], lat[1, second], lat[2, first], lat[3, second]], axis=0
            )
            at = pl.multiple_of(row_of(xx, yy, zz) * TOK, TOK)
            pair = jnp.dot(wkt[...], tokens, preferred_element_type=F32)
            keys_t[:, pl.ds(at, TOK)] = pair[:HEAD].astype(BF16)
            values[pl.ds(at, TOK), :HEAD] = pair[HEAD:].T.astype(BF16)
        return carry

    def last_group(j):
        for half in (0, 1):
            lat_copy(half, 15 + j).wait_recv()
            lat_copy(half, 19 + j).wait_recv()
            sib_copy(half, 3, j).start()

    lax.fori_loop(0, 3, project, 0)
    last_group(0)
    lax.fori_loop(3, 6, project, 0)
    last_group(1)
    out_stage(0)
    lax.fori_loop(6, 9, project, 0)

    def last_handed(j):
        for half in (0, 1):
            sib_copy(half, 3, j).wait_recv()

    last_handed(0)
    lax.fori_loop(9, 11, project, 0)
    last_group(2)
    last_handed(1)
    lax.fori_loop(11, 13, project, 0)
    last_group(3)
    last_handed(2)
    lax.fori_loop(13, 15, project, 0)
    last_handed(3)
    project(15, 0)

    att_place = feats.at[
        col,
        pl.ds(pl.multiple_of(row // 4 * STRIPE, STRIPE), STRIPE),
        pl.ds(pl.multiple_of(head_local * HEAD, HEAD), HEAD),
    ]

    def att_copy(r, d):
        return remote(att.at[r], att_place, hs.at[d], hr.at[d], (r, col))

    local_att = pltpu.make_async_copy(att.at[row], att_place, ls.at[4])

    def place_of(h, k):
        return h * 2 + k

    def feat_copy(n, part):
        lanes = pl.ds(pl.multiple_of(part * 256, 256), 256)

        def at(place, first, count):
            return feats.at[place, pl.ds(first, count), lanes]

        if n == 0:
            src, to = at(col, 0, TOK), place_of(up(zh), core)
        elif n == 1:
            src, to = at(col, 0, TOK), place_of(down(zh), core)
        elif n == 2:
            src, to = at(col, 0, TOK), place_of(zh, 1 - core)
        elif n == 3:
            src, to = at(place_of(down(zh), core), 0, 192), place_of(up(zh), core)
        elif n == 4:
            src, to = at(place_of(up(zh), core), 192, 192), place_of(down(zh), core)
        elif n == 5:
            src, to = at(place_of(down(zh), core), 0, TOK), place_of(zh, 1 - core)
        elif n == 6:
            src, to = at(place_of(up(zh), core), 0, TOK), place_of(zh, 1 - core)
        else:
            src, to = at(place_of(across(zh), core), 0, TOK), place_of(zh, 1 - core)
        return remote(src, src, zs.at[part, n], zr.at[part, n], (row, to))

    def feat_start(part):
        @pl.when(head_local // 2 == part)
        def _():
            local_att.start()

        def arrival(j, carry):
            source = j // 2 * 4 + part * 2 + lax.rem(j, 2)

            @pl.when(source != row)
            def _():
                att_copy(row, lax.rem(source - row + ROWS, ROWS)).wait_recv()

            return carry

        lax.fori_loop(0, ROWS // 2, arrival, 0)

        @pl.when(head_local // 2 == part)
        def _():
            local_att.wait()

        for n in range(3):
            feat_copy(n, part).start()

    def feat_forward(part):
        feat_copy(0, part).wait_recv()
        feat_copy(3, part).start()
        feat_copy(5, part).start()
        feat_copy(1, part).wait_recv()
        feat_copy(4, part).start()
        feat_copy(6, part).start()

    def feat_hand_over(part):
        feat_copy(3, part).wait_recv()
        feat_copy(4, part).wait_recv()
        feat_copy(7, part).start()

    turned = head_local // 2
    my_block = row // QROWS
    early = jnp.where(my_block == 3, 1, 0)

    def beside(tick):
        for after in range(1, 5):

            @pl.when(tick == after + 1)
            def _(after=after):
                out_stage(after)

        @pl.when(
            ((tick == 2) & (my_block == 0))
            | ((tick == 3) & (my_block == 1))
            | ((tick == 4) & (my_block == 3))
            | ((tick == 5) & (my_block == 2))
        )
        def _():
            feat_start(early)

        @pl.when(((tick == 4) & (my_block == 0)) | ((tick == 5) & (my_block == 1)))
        def _():
            feat_start(1 - early)

    def turn(query, start, first_key, keys, allowed):
        scores = jnp.dot(
            query[start:], keys_t[:, pl.ds(first_key, keys)], preferred_element_type=F32
        )
        if allowed is not None:
            scores = jnp.where(allowed, scores, NEG_FILL)
        before = top[start:, :1]
        now = jnp.maximum(before, jnp.max(scores, axis=1, keepdims=True))
        weights = jnp.exp2((scores - now) * SCALE).astype(BF16)
        rescale = jnp.exp2((before - now) * SCALE)
        acc[start:, :] = acc[start:, :] * rescale + jnp.dot(
            weights, values[pl.ds(first_key, keys), :], preferred_element_type=F32
        )
        top[start:, :] = jnp.broadcast_to(now, (QB - start, HEAD))

    def attend(turn_index, carry):
        block = lax.rem(turn_index + 3 * turned, BLOCKS)
        before = jnp.where(
            turned == 0,
            turn_index * (turn_index - 1) // 2,
            jnp.where(turn_index >= 2, turn_index + 1, 0),
        )
        query = queries[pl.ds(block * QROWS, QROWS)].reshape(QB, HEAD)
        acc[...] = jnp.zeros_like(acc)
        top[...] = jnp.full(top.shape, NEG_FILL, F32)

        def full(step, inner):
            beside(before + step)
            turn(query, 0, pl.multiple_of(step * KB, KB), KB, None)
            return inner

        lax.fori_loop(0, block, full, 0)
        for part in range(QROWS // DIAG):
            start = part * DIAG * STRIPE
            shape = (QB - start, DIAG * TOK)
            place = lax.broadcasted_iota(jnp.int32, shape, 0)
            key = lax.broadcasted_iota(jnp.int32, shape, 1)
            source = sum(
                (place >= STRIPE * j).astype(jnp.int32) for j in range(1, QROWS - part * DIAG)
            )
            position = source * (TOK - STRIPE) + place + row // 4 * STRIPE
            first_key = pl.multiple_of(block * KB + part * DIAG * TOK, DIAG * TOK)
            turn(query, start, first_key, DIAG * TOK, key <= position)
        done = (acc[:, :HEAD] / acc[:, HEAD:]).astype(BF16)
        att[pl.ds(block * QROWS, QROWS)] = done.reshape(QROWS, STRIPE, HEAD)
        for j in range(QROWS):
            r = block * QROWS + j

            @pl.when(r != row)
            def _(r=r):
                att_copy(r, lax.rem(row - r + ROWS, ROWS)).start()

        return carry

    lax.fori_loop(0, BLOCKS, attend, 0)

    @pl.when(my_block >= 2)
    def _():
        feat_start(1 - early)

    out_stage(5)

    feat_forward(early)

    feat_forward(1 - early)
    feat_hand_over(early)
    for half in (0, 1):
        for n in range(13, 21):
            out_copy(half, n).wait_recv()

    def mix(c, part, first=False):
        low = c // 4
        within = lax.rem(c, 4)
        weights = []
        for j in (0, 1):
            xx = part * 2 + j
            weights.append(wout[low, jnp.where(low == 0, xx * 4 + within, within * 4 + xx)])
        heads = feats[c, :, pl.ds(pl.multiple_of(part * 256, 256), 256)]
        product = jnp.dot(heads, jnp.concatenate(weights, axis=0), preferred_element_type=F32)
        if first:
            total[...] = product
        else:
            total[...] += product

    def mix_some(n, part):
        h = jnp.where(n == 0, zh, jnp.where(lax.rem(n, 2) == 1, down(zh), up(zh)))
        k = jnp.where((n == 1) | (n == 2), core, 1 - core)
        mix(place_of(h, k), part)
        return part

    mix(col, early, True)
    for part in (early, 1 - early):
        if part is not early:
            mix(col, part)
        feat_copy(2, part).wait_recv()
        lax.fori_loop(0, 3, mix_some, part)
        feat_copy(5, part).wait_recv()
        feat_copy(6, part).wait_recv()
        lax.fori_loop(3, 5, mix_some, part)
        if part is not early:
            feat_hand_over(part)
        mix(place_of(across(zh), core), part)
        feat_copy(7, part).wait_recv()
        mix(place_of(across(zh), 1 - core), part)
    out_ref[...] = total[...].astype(BF16)

    for d in (1, 2, 3):
        col_copy(d).wait_send()
    for half in (0, 1):
        for n in range(23):
            lat_copy(half, n).wait_send()
        for g in range(4):
            for j in range(4):
                sib_copy(half, g, j).wait_send()
        for n in range(1, 21):
            out_copy(half, n).wait_send()
    out_first.wait_send()

    def att_sent(d, carry):
        att_copy(lax.rem(row - d + ROWS, ROWS), d).wait_send()
        return carry

    lax.fori_loop(1, ROWS, att_sent, 0)
    for part in (0, 1):
        for n in range(8):
            feat_copy(n, part).wait_send()


def per_device(latent, w_kv, queries, w_out):
    dma = pltpu.SemaphoreType.DMA
    vmem = pltpu.VMEM
    return pl.pallas_call(
        kernel,
        out_shape=jax.ShapeDtypeStruct((TOK, w_out.shape[1]), BF16),
        in_specs=[pl.BlockSpec(memory_space=pltpu.VMEM)] * 4,
        out_specs=pl.BlockSpec(memory_space=pltpu.VMEM),
        scratch_shapes=[
            vmem((4, ROWS, 128, TOK), BF16),
            vmem((ROWS, 16, 256), BF16),
            vmem((256, 512), BF16),
            vmem((ROWS, STRIPE, HEAD), BF16),
            vmem((HEAD, ROWS * TOK), BF16),
            vmem((ROWS * TOK, 256), BF16),
            vmem((ROWS, STRIPE, HEAD), BF16),
            vmem((8, TOK, 512), BF16),
            vmem((2, 16, 128, 896), BF16),
            vmem((QB, 256), F32),
            vmem((QB, 128), F32),
            vmem((TOK, 896), F32),
            dma((4,)), dma((4,)),
            dma((ROWS,)), dma((ROWS,)),
            dma((ROWS,)), dma((ROWS,)),
            dma((2, 23)), dma((2, 23)),
            dma((2, 16)), dma((2, 16)),
            dma((2, 21)), dma((2, 21)),
            dma((ROWS,)), dma((ROWS,)),
            dma((2, 8)), dma((2, 8)),
            dma((5,)),
        ],
        compiler_params=pltpu.CompilerParams(
            collective_id=0, has_side_effects=True, vmem_limit_bytes=60 * 1024 * 1024
        ),
        cost_estimate=pl.CostEstimate(
            flops=12_000_000_000, bytes_accessed=2_000_000, transcendentals=11_000_000
        ),
    )(latent.T, w_kv, queries, w_out)


def solution(mesh):
    spec = P("row", "col")
    return jax.shard_map(
        per_device, mesh=mesh, in_specs=(spec,) * 4, out_specs=spec, check_vma=False
    )
```

```python
import functools

import jax
import jax.numpy as jnp
from jax import lax
from jax.experimental import pallas as pl
from jax.experimental.pallas import tpu as pltpu
from jax.sharding import PartitionSpec as P

HEAD = 128
NEG_FILL = -1e30
MESH = pl.DeviceIdType.MESH
BF16 = jnp.bfloat16
F32 = jnp.float32

ROWS = 32
TOK = 384
STRIPE = 48
QROWS = 8
DIAG = 4
QB = QROWS * STRIPE
KB = QROWS * TOK
BLOCKS = ROWS // QROWS
SCALE = HEAD**-0.5 * 1.4426950408889634


def kernel(
    lat_ref, wkv_ref, q_ref, wout_ref, out_ref,
    lat, wkv, wkt, queries, keys_t, values, att, feats, wout, acc, top, total,
    cs, cr, qs, qr, ws, wr, gs, gr, ss, sr, os, orr, hs, hr, zs, zr, ls,
):
    row = lax.axis_index("row")
    col = lax.axis_index("col")
    x = lax.rem(row, 4)
    y = lax.rem(row // 4, 4)
    zl = row // 16
    zh = col // 2
    core = lax.rem(col, 2)
    sibling = (row, zh * 2 + 1 - core)

    def row_of(xx, yy, zz):
        return zz * 16 + yy * 4 + xx

    def up(v):
        return lax.rem(v + 1, 4)

    def down(v):
        return lax.rem(v + 3, 4)

    def across(v):
        return lax.rem(v + 2, 4)

    def remote(src, dst, send, recv, device):
        return pltpu.make_async_remote_copy(
            src_ref=src, dst_ref=dst, send_sem=send, recv_sem=recv,
            device_id=device, device_id_type=MESH,
        )

    barrier = pltpu.get_barrier_semaphore()

    def greet_row(d, carry):
        pl.semaphore_signal(
            barrier, inc=1, device_id=(lax.rem(row + d, ROWS), col), device_id_type=MESH
        )
        return carry

    def greet_col(d, carry):
        pl.semaphore_signal(
            barrier, inc=1, device_id=(row, lax.rem(col + d, 8)), device_id_type=MESH
        )
        return carry

    lax.fori_loop(1, 8, greet_col, 0)
    lax.fori_loop(1, ROWS, greet_row, 0)
    pl.semaphore_wait(barrier, ROWS - 1 + 7)

    home = zh // 2
    own_slot = lax.rem(zh, 2) * 2 + core
    slots = ((x * 4 + y) * 2 + zl, (y * 4 + x) * 2 + zl)
    own_place = lat.at[
        zh,
        jnp.where(lax.rem(zh, 2) == 0, slots[0], slots[1]),
        pl.ds(pl.multiple_of(core * 64, 64), 64),
    ]

    def col_copy(d):
        dst = (row, lax.rem(zh + d, 4) * 2 + home)
        return remote(lat_ref, own_place, cs.at[d], cr.at[own_slot], dst)

    for d in (2, 1, 3):
        col_copy(d).start()

    @pl.when(core != home)
    def _():
        col_copy(0).start()

    own_piece = pltpu.make_async_copy(lat_ref, own_place, ls.at[0])

    @pl.when(core == home)
    def _():
        own_piece.start()

    head_local = x

    def q_part(peer):
        return q_ref.at[
            pl.ds(pl.multiple_of(peer // 4 * STRIPE, STRIPE), STRIPE),
            pl.ds(pl.multiple_of(lax.rem(peer, 4) * HEAD, HEAD), HEAD),
        ]

    def w_part(peer):
        return wkv_ref.at[:, pl.ds(pl.multiple_of(lax.rem(peer, 4) * 256, 256), 256)]

    def q_copy(d):
        peer = lax.rem(row + d, ROWS)
        return remote(q_part(peer), queries.at[row], qs.at[d], qr.at[d], (peer, col))

    def w_copy(d):
        peer = lax.rem(row + d, ROWS)
        return remote(w_part(peer), wkv.at[row], ws.at[d], wr.at[d], (peer, col))

    def small_start(d, carry):
        w_copy(d).start()
        q_copy(d).start()
        return carry

    def axes(half):
        if half == 0:
            return x, y, lambda aa, bb, zz: row_of(aa, bb, zz)
        return y, x, lambda aa, bb, zz: row_of(bb, aa, zz)

    def lat_copy(half, n):
        a, b, dev = axes(half)
        buf = lat.at[core * 2 + half]
        across_b = (b, down(b), up(b), across(b))

        def at(aa, bb, zz, count):
            return buf.at[pl.ds((aa * 4 + bb) * 2 + zz, count)]

        if n == 0:
            src, to = at(a, b, zl, 1), dev(a, b, 1 - zl)
        elif n <= 4:
            src = at(a, b, zl if n <= 2 else 1 - zl, 1)
            to = dev(a, up(b) if n % 2 == 1 else down(b), zl)
        elif n == 5:
            src, to = at(a, down(b), zl, 1), dev(a, up(b), zl)
        elif n == 6:
            src, to = at(a, up(b), 1 - zl, 1), dev(a, down(b), zl)
        elif n < 11:
            src, to = at(a, across_b[n - 7], 0, 2), dev(up(a), b, zl)
        elif n < 15:
            src, to = at(a, across_b[n - 11], 0, 2), dev(down(a), b, zl)
        elif n < 19:
            src, to = at(down(a), across_b[n - 15], 0, 1), dev(up(a), b, zl)
        else:
            src, to = at(up(a), across_b[n - 19], 1, 1), dev(down(a), b, zl)
        return remote(src, src, gs.at[half, n], gr.at[half, n], (to, col))

    def sib_copy(half, g, j):
        a, b, _ = axes(half)
        aa = (a, down(a), up(a), across(a))[g]
        bb = (b, down(b), up(b), across(b))[j]
        src = lat.at[core * 2 + half, pl.ds((aa * 4 + bb) * 2, 2)]
        return remote(src, src, ss.at[half, g * 4 + j], sr.at[half, g * 4 + j], sibling)

    def out_copy(half, n):
        a, b, dev = axes(half)
        buf = wout.at[half]
        across_b = (b, down(b), up(b), across(b))
        if n <= 2:
            src = buf.at[a * 4 + b]
            to = dev(a, up(b) if n == 1 else down(b), zl)
        elif n == 3:
            src, to = buf.at[a * 4 + down(b), pl.ds(0, 64)], dev(a, up(b), zl)
        elif n == 4:
            src, to = buf.at[a * 4 + up(b), pl.ds(64, 64)], dev(a, down(b), zl)
        elif n < 9:
            src, to = buf.at[a * 4 + across_b[n - 5]], dev(up(a), b, zl)
        elif n < 13:
            src, to = buf.at[a * 4 + across_b[n - 9]], dev(down(a), b, zl)
        elif n < 17:
            src, to = buf.at[down(a) * 4 + across_b[n - 13], pl.ds(0, 64)], dev(up(a), b, zl)
        else:
            src, to = buf.at[up(a) * 4 + across_b[n - 17], pl.ds(64, 64)], dev(down(a), b, zl)
        return remote(src, src, os.at[half, n], orr.at[half, n], (to, col))

    def out_step(half, landed, sent):
        for n in landed:
            out_copy(half, n).wait_recv()
        for n in sent:
            out_copy(half, n).start()

    first_steps = {
        0: [((1,), (3, 6, 10)), ((2,), (4, 7, 11)), ((5,), (13,)), ((9,), (17,))],
        1: [((3, 4), (8, 12)), ((6,), (14,)), ((10,), (18,))],
        2: [((7,), (15,)), ((11,), (19,))],
        3: [((8,), (16,)), ((12,), (20,))],
    }
    second_steps = {
        0: [((), (1, 2, 5, 9))],
        1: [((1,), (3, 6, 10)), ((2,), (4, 7, 11))],
        2: [((5,), (13,)), ((9,), (17,))],
        3: [((3, 4), (8, 12)), ((6,), (14,)), ((10,), (18,))],
        4: [((7,), (15,)), ((11,), (19,))],
        5: [((8,), (16,)), ((12,), (20,))],
    }

    def out_stage(stage):
        if stage == 0:
            out_first.wait_recv()
        for steps, own in ((second_steps, False), (first_steps, True)):
            for half in (0, 1):

                @pl.when((zl == half) if own else (zl != half))
                def _(half=half, steps=steps):
                    for landed, sent in steps.get(stage, []):
                        out_step(half, landed, sent)

    own_out = wout.at[zl, jnp.where(zl == 0, x * 4 + y, y * 4 + x)]
    out_first = remote(wout_ref, own_out, os.at[0, 0], orr.at[0, 0], (row_of(x, y, 1 - zl), col))
    out_local = pltpu.make_async_copy(wout_ref, own_out, ls.at[3])

    lax.fori_loop(1, ROWS, small_start, 0)
    local_q = pltpu.make_async_copy(q_part(row), queries.at[row], ls.at[1])
    local_w = pltpu.make_async_copy(w_part(row), wkv.at[row], ls.at[2])
    local_q.start()
    local_w.start()
    out_local.start()
    out_local.wait()
    for half in (0, 1):

        @pl.when(zl == half)
        def _(half=half):
            for n in (1, 2, 5, 9):
                out_copy(half, n).start()

    @pl.when(core != home)
    def _():
        col_copy(0).wait_send()

    @pl.when(core == home)
    def _():
        own_piece.wait()

    def piece_arrival(slot):
        return remote(lat_ref, own_place, cs.at[0], cr.at[slot], sibling)

    for slot in range(4):

        @pl.when(jnp.logical_not((core == home) & (own_slot == slot)))
        def _(slot=slot):
            piece_arrival(slot).wait_recv()

    for half in (0, 1):
        for n in (0, 1, 2):
            lat_copy(half, n).start()
    for half in (0, 1):
        lat_copy(half, 0).wait_recv()
        for n in (3, 4, 7, 11):
            lat_copy(half, n).start()
        sib_copy(half, 0, 0).start()
    out_first.start()
    for half in (0, 1):
        lat_copy(half, 1).wait_recv()
        lat_copy(half, 5).start()
        lat_copy(half, 4).wait_recv()
        lat_copy(half, 6).start()
    for half in (0, 1):
        lat_copy(half, 3).wait_recv()
        for n in (8, 12):
            lat_copy(half, n).start()
        sib_copy(half, 0, 1).start()
        lat_copy(half, 2).wait_recv()
        for n in (9, 13):
            lat_copy(half, n).start()
        sib_copy(half, 0, 2).start()
    for half in (0, 1):
        lat_copy(half, 5).wait_recv()
        lat_copy(half, 6).wait_recv()
        for n in (10, 14):
            lat_copy(half, n).start()
        sib_copy(half, 0, 3).start()

    def small_wait(d, carry):
        w_copy(d).wait()
        q_copy(d).wait()
        return carry

    lax.fori_loop(1, ROWS, small_wait, 0)
    local_q.wait()
    local_w.wait()
    wkt[...] = wkv[...].reshape(512, 256).T
    values[:, HEAD:] = jnp.ones((ROWS * TOK, HEAD), BF16)

    for j in range(4):
        for half in (0, 1):
            lat_copy(half, 7 + j).wait_recv()
            lat_copy(half, 15 + j).start()
            sib_copy(half, 1, j).start()
            lat_copy(half, 11 + j).wait_recv()
            lat_copy(half, 19 + j).start()
            sib_copy(half, 2, j).start()
    for half in (0, 1):
        for g in range(3):
            for j in range(4):
                sib_copy(half, g, j).wait_recv()

    def project(i, carry):
        later = i - 9
        j = later // 2
        beyond = jnp.where(j == 0, 0, jnp.where(j == 1, 3, jnp.where(j == 2, 1, 2)))
        even = lax.rem(later + 10, 2) == 0
        xx = jnp.where(i < 9, x + lax.rem(i, 3) + 3, jnp.where(even, x + 2, x + beyond))
        yy = jnp.where(i < 9, y + i // 3 + 3, jnp.where(even, y + beyond, y + 2))
        xx = lax.rem(xx, 4)
        yy = lax.rem(yy, 4)
        for zz in (0, 1):
            first = (xx * 4 + yy) * 2 + zz
            second = (yy * 4 + xx) * 2 + zz
            tokens = jnp.concatenate(
                [lat[0, first], lat[1, second], lat[2, first], lat[3, second]], axis=0
            )
            at = pl.multiple_of(row_of(xx, yy, zz) * TOK, TOK)
            pair = jnp.dot(wkt[...], tokens, preferred_element_type=F32)
            keys_t[:, pl.ds(at, TOK)] = pair[:HEAD].astype(BF16)
            values[pl.ds(at, TOK), :HEAD] = pair[HEAD:].T.astype(BF16)
        return carry

    def last_group(j):
        for half in (0, 1):
            lat_copy(half, 15 + j).wait_recv()
            lat_copy(half, 19 + j).wait_recv()
            sib_copy(half, 3, j).start()

    lax.fori_loop(0, 3, project, 0)
    last_group(0)
    lax.fori_loop(3, 6, project, 0)
    last_group(1)
    out_stage(0)
    lax.fori_loop(6, 9, project, 0)

    def last_handed(j):
        for half in (0, 1):
            sib_copy(half, 3, j).wait_recv()

    last_handed(0)
    lax.fori_loop(9, 11, project, 0)
    last_group(2)
    last_handed(1)
    lax.fori_loop(11, 13, project, 0)
    last_group(3)
    last_handed(2)
    lax.fori_loop(13, 15, project, 0)
    last_handed(3)
    project(15, 0)

    att_place = feats.at[
        col,
        pl.ds(pl.multiple_of(row // 4 * STRIPE, STRIPE), STRIPE),
        pl.ds(pl.multiple_of(head_local * HEAD, HEAD), HEAD),
    ]

    def att_copy(r, d):
        return remote(att.at[r], att_place, hs.at[d], hr.at[d], (r, col))

    local_att = pltpu.make_async_copy(att.at[row], att_place, ls.at[4])

    def place_of(h, k):
        return h * 2 + k

    def feat_copy(n, part):
        lanes = pl.ds(pl.multiple_of(part * 256, 256), 256)

        def at(place, first, count):
            return feats.at[place, pl.ds(first, count), lanes]

        if n == 0:
            src, to = at(col, 0, TOK), place_of(up(zh), core)
        elif n == 1:
            src, to = at(col, 0, TOK), place_of(down(zh), core)
        elif n == 2:
            src, to = at(col, 0, TOK), place_of(zh, 1 - core)
        elif n == 3:
            src, to = at(place_of(down(zh), core), 0, 192), place_of(up(zh), core)
        elif n == 4:
            src, to = at(place_of(up(zh), core), 192, 192), place_of(down(zh), core)
        elif n == 5:
            src, to = at(place_of(down(zh), core), 0, TOK), place_of(zh, 1 - core)
        elif n == 6:
            src, to = at(place_of(up(zh), core), 0, TOK), place_of(zh, 1 - core)
        else:
            src, to = at(place_of(across(zh), core), 0, TOK), place_of(zh, 1 - core)
        return remote(src, src, zs.at[part, n], zr.at[part, n], (row, to))

    def feat_start(part):
        @pl.when(head_local // 2 == part)
        def _():
            local_att.start()

        def arrival(j, carry):
            source = j // 2 * 4 + part * 2 + lax.rem(j, 2)

            @pl.when(source != row)
            def _():
                att_copy(row, lax.rem(source - row + ROWS, ROWS)).wait_recv()

            return carry

        lax.fori_loop(0, ROWS // 2, arrival, 0)

        @pl.when(head_local // 2 == part)
        def _():
            local_att.wait()

        for n in range(3):
            feat_copy(n, part).start()

    def feat_forward(part):
        feat_copy(0, part).wait_recv()
        feat_copy(3, part).start()
        feat_copy(5, part).start()
        feat_copy(1, part).wait_recv()
        feat_copy(4, part).start()
        feat_copy(6, part).start()

    def feat_hand_over(part):
        feat_copy(3, part).wait_recv()
        feat_copy(4, part).wait_recv()
        feat_copy(7, part).start()

    turned = head_local // 2
    my_block = row // QROWS
    early = jnp.where(my_block == 3, 1, 0)

    def beside(tick):
        for after in range(1, 5):

            @pl.when(tick == after + 1)
            def _(after=after):
                out_stage(after)

        @pl.when(
            ((tick == 2) & (my_block == 0))
            | ((tick == 3) & (my_block == 1))
            | ((tick == 4) & (my_block == 3))
            | ((tick == 4) & (my_block == 2))
        )
        def _():
            feat_start(early)

        @pl.when((tick == 5) & (my_block == 0))
        def _():
            feat_forward(early)

        @pl.when(((tick == 4) & (my_block == 0)) | ((tick == 5) & (my_block == 1)))
        def _():
            feat_start(1 - early)

    def turn(query, start, first_key, keys, allowed):
        scores = jnp.dot(
            query[start:], keys_t[:, pl.ds(first_key, keys)], preferred_element_type=F32
        )
        if allowed is not None:
            scores = jnp.where(allowed, scores, NEG_FILL)
        before = top[start:, :1]
        now = jnp.maximum(before, jnp.max(scores, axis=1, keepdims=True))
        weights = jnp.exp2((scores - now) * SCALE).astype(BF16)
        rescale = jnp.exp2((before - now) * SCALE)
        acc[start:, :] = acc[start:, :] * rescale + jnp.dot(
            weights, values[pl.ds(first_key, keys), :], preferred_element_type=F32
        )
        top[start:, :] = jnp.broadcast_to(now, (QB - start, HEAD))

    def attend(turn_index, carry):
        block = lax.rem(turn_index + 3 * turned, BLOCKS)
        before = jnp.where(
            turned == 0,
            turn_index * (turn_index - 1) // 2,
            jnp.where(turn_index >= 2, turn_index + 1, 0),
        )
        query = queries[pl.ds(block * QROWS, QROWS)].reshape(QB, HEAD)
        acc[...] = jnp.zeros_like(acc)
        top[...] = jnp.full(top.shape, NEG_FILL, F32)

        def full(step, inner):
            beside(before + step)
            turn(query, 0, pl.multiple_of(step * KB, KB), KB, None)
            return inner

        lax.fori_loop(0, block, full, 0)
        for part in range(QROWS // DIAG):
            start = part * DIAG * STRIPE
            shape = (QB - start, DIAG * TOK)
            place = lax.broadcasted_iota(jnp.int32, shape, 0)
            key = lax.broadcasted_iota(jnp.int32, shape, 1)
            source = sum(
                (place >= STRIPE * j).astype(jnp.int32) for j in range(1, QROWS - part * DIAG)
            )
            position = source * (TOK - STRIPE) + place + row // 4 * STRIPE
            first_key = pl.multiple_of(block * KB + part * DIAG * TOK, DIAG * TOK)
            turn(query, start, first_key, DIAG * TOK, key <= position)
        done = (acc[:, :HEAD] / acc[:, HEAD:]).astype(BF16)
        att[pl.ds(block * QROWS, QROWS)] = done.reshape(QROWS, STRIPE, HEAD)
        for j in range(QROWS):
            r = block * QROWS + j

            @pl.when(r != row)
            def _(r=r):
                att_copy(r, lax.rem(row - r + ROWS, ROWS)).start()

        return carry

    lax.fori_loop(0, BLOCKS, attend, 0)

    @pl.when(my_block >= 2)
    def _():
        feat_start(1 - early)

    out_stage(5)

    @pl.when(my_block != 0)
    def _():
        feat_forward(early)

    feat_forward(1 - early)
    feat_hand_over(early)
    for half in (0, 1):
        for n in range(13, 21):
            out_copy(half, n).wait_recv()

    def mix(c, part, first=False):
        low = c // 4
        within = lax.rem(c, 4)
        weights = []
        for j in (0, 1):
            xx = part * 2 + j
            weights.append(wout[low, jnp.where(low == 0, xx * 4 + within, within * 4 + xx)])
        heads = feats[c, :, pl.ds(pl.multiple_of(part * 256, 256), 256)]
        product = jnp.dot(heads, jnp.concatenate(weights, axis=0), preferred_element_type=F32)
        if first:
            total[...] = product
        else:
            total[...] += product

    def mix_some(n, part):
        h = jnp.where(n == 0, zh, jnp.where(lax.rem(n, 2) == 1, down(zh), up(zh)))
        k = jnp.where((n == 1) | (n == 2), core, 1 - core)
        mix(place_of(h, k), part)
        return part

    mix(col, early, True)
    for part in (early, 1 - early):
        if part is not early:
            mix(col, part)
        feat_copy(2, part).wait_recv()
        lax.fori_loop(0, 3, mix_some, part)
        feat_copy(5, part).wait_recv()
        feat_copy(6, part).wait_recv()
        lax.fori_loop(3, 5, mix_some, part)
        if part is not early:
            feat_hand_over(part)
        mix(place_of(across(zh), core), part)
        feat_copy(7, part).wait_recv()
        mix(place_of(across(zh), 1 - core), part)
    out_ref[...] = total[...].astype(BF16)

    for d in (1, 2, 3):
        col_copy(d).wait_send()
    for half in (0, 1):
        for n in range(23):
            lat_copy(half, n).wait_send()
        for g in range(4):
            for j in range(4):
                sib_copy(half, g, j).wait_send()
        for n in range(1, 21):
            out_copy(half, n).wait_send()
    out_first.wait_send()

    def att_sent(d, carry):
        att_copy(lax.rem(row - d + ROWS, ROWS), d).wait_send()
        return carry

    lax.fori_loop(1, ROWS, att_sent, 0)
    for part in (0, 1):
        for n in range(8):
            feat_copy(n, part).wait_send()


def per_device(latent, w_kv, queries, w_out):
    dma = pltpu.SemaphoreType.DMA
    vmem = pltpu.VMEM
    return pl.pallas_call(
        kernel,
        out_shape=jax.ShapeDtypeStruct((TOK, w_out.shape[1]), BF16),
        in_specs=[pl.BlockSpec(memory_space=pltpu.VMEM)] * 4,
        out_specs=pl.BlockSpec(memory_space=pltpu.VMEM),
        scratch_shapes=[
            vmem((4, ROWS, 128, TOK), BF16),
            vmem((ROWS, 16, 256), BF16),
            vmem((256, 512), BF16),
            vmem((ROWS, STRIPE, HEAD), BF16),
            vmem((HEAD, ROWS * TOK), BF16),
            vmem((ROWS * TOK, 256), BF16),
            vmem((ROWS, STRIPE, HEAD), BF16),
            vmem((8, TOK, 512), BF16),
            vmem((2, 16, 128, 896), BF16),
            vmem((QB, 256), F32),
            vmem((QB, 128), F32),
            vmem((TOK, 896), F32),
            dma((4,)), dma((4,)),
            dma((ROWS,)), dma((ROWS,)),
            dma((ROWS,)), dma((ROWS,)),
            dma((2, 23)), dma((2, 23)),
            dma((2, 16)), dma((2, 16)),
            dma((2, 21)), dma((2, 21)),
            dma((ROWS,)), dma((ROWS,)),
            dma((2, 8)), dma((2, 8)),
            dma((5,)),
        ],
        compiler_params=pltpu.CompilerParams(
            collective_id=0, has_side_effects=True, vmem_limit_bytes=60 * 1024 * 1024
        ),
        cost_estimate=pl.CostEstimate(
            flops=12_000_000_000, bytes_accessed=2_000_000, transcendentals=11_000_000
        ),
    )(latent.T, w_kv, queries, w_out)


def solution(mesh):
    spec = P("row", "col")
    return jax.shard_map(
        per_device, mesh=mesh, in_specs=(spec,) * 4, out_specs=spec, check_vma=False
    )
```

```python
import functools

import jax
import jax.numpy as jnp
from jax import lax
from jax.experimental import pallas as pl
from jax.experimental.pallas import tpu as pltpu
from jax.sharding import PartitionSpec as P

HEAD = 128
NEG_FILL = -1e30
MESH = pl.DeviceIdType.MESH
BF16 = jnp.bfloat16
F32 = jnp.float32

ROWS = 32
TOK = 384
STRIPE = 48
QROWS = 8
DIAG = 4
QB = QROWS * STRIPE
KB = QROWS * TOK
BLOCKS = ROWS // QROWS
SCALE = HEAD**-0.5 * 1.4426950408889634


def kernel(
    lat_ref, wkv_ref, q_ref, wout_ref, out_ref,
    lat, wkv, wkt, queries, keys_t, values, att, feats, wout, acc, top, total,
    cs, cr, qs, qr, ws, wr, gs, gr, ss, sr, os, orr, hs, hr, zs, zr, ls,
):
    row = lax.axis_index("row")
    col = lax.axis_index("col")
    x = lax.rem(row, 4)
    y = lax.rem(row // 4, 4)
    zl = row // 16
    zh = col // 2
    core = lax.rem(col, 2)
    sibling = (row, zh * 2 + 1 - core)

    def row_of(xx, yy, zz):
        return zz * 16 + yy * 4 + xx

    def up(v):
        return lax.rem(v + 1, 4)

    def down(v):
        return lax.rem(v + 3, 4)

    def across(v):
        return lax.rem(v + 2, 4)

    def remote(src, dst, send, recv, device):
        return pltpu.make_async_remote_copy(
            src_ref=src, dst_ref=dst, send_sem=send, recv_sem=recv,
            device_id=device, device_id_type=MESH,
        )

    barrier = pltpu.get_barrier_semaphore()

    def greet_row(d, carry):
        pl.semaphore_signal(
            barrier, inc=1, device_id=(lax.rem(row + d, ROWS), col), device_id_type=MESH
        )
        return carry

    def greet_col(d, carry):
        pl.semaphore_signal(
            barrier, inc=1, device_id=(row, lax.rem(col + d, 8)), device_id_type=MESH
        )
        return carry

    lax.fori_loop(1, 8, greet_col, 0)
    lax.fori_loop(1, ROWS, greet_row, 0)
    pl.semaphore_wait(barrier, ROWS - 1 + 7)

    home = zh // 2
    own_slot = lax.rem(zh, 2) * 2 + core
    slots = ((x * 4 + y) * 2 + zl, (y * 4 + x) * 2 + zl)
    own_place = lat.at[
        zh,
        jnp.where(lax.rem(zh, 2) == 0, slots[0], slots[1]),
        pl.ds(pl.multiple_of(core * 64, 64), 64),
    ]

    def col_copy(d):
        dst = (row, lax.rem(zh + d, 4) * 2 + home)
        return remote(lat_ref, own_place, cs.at[d], cr.at[own_slot], dst)

    for d in (2, 1, 3):
        col_copy(d).start()

    @pl.when(core != home)
    def _():
        col_copy(0).start()

    own_piece = pltpu.make_async_copy(lat_ref, own_place, ls.at[0])

    @pl.when(core == home)
    def _():
        own_piece.start()

    head_local = x

    def q_part(peer):
        return q_ref.at[
            pl.ds(pl.multiple_of(peer // 4 * STRIPE, STRIPE), STRIPE),
            pl.ds(pl.multiple_of(lax.rem(peer, 4) * HEAD, HEAD), HEAD),
        ]

    def w_part(peer):
        return wkv_ref.at[:, pl.ds(pl.multiple_of(lax.rem(peer, 4) * 256, 256), 256)]

    def q_copy(d):
        peer = lax.rem(row + d, ROWS)
        return remote(q_part(peer), queries.at[row], qs.at[d], qr.at[d], (peer, col))

    def w_copy(d):
        peer = lax.rem(row + d, ROWS)
        return remote(w_part(peer), wkv.at[row], ws.at[d], wr.at[d], (peer, col))

    def small_start(d, carry):
        w_copy(d).start()
        q_copy(d).start()
        return carry

    def axes(half):
        if half == 0:
            return x, y, lambda aa, bb, zz: row_of(aa, bb, zz)
        return y, x, lambda aa, bb, zz: row_of(bb, aa, zz)

    def lat_copy(half, n):
        a, b, dev = axes(half)
        buf = lat.at[core * 2 + half]
        across_b = (b, down(b), up(b), across(b))

        def at(aa, bb, zz, count):
            return buf.at[pl.ds((aa * 4 + bb) * 2 + zz, count)]

        if n == 0:
            src, to = at(a, b, zl, 1), dev(a, b, 1 - zl)
        elif n <= 4:
            src = at(a, b, zl if n <= 2 else 1 - zl, 1)
            to = dev(a, up(b) if n % 2 == 1 else down(b), zl)
        elif n == 5:
            src, to = at(a, down(b), zl, 1), dev(a, up(b), zl)
        elif n == 6:
            src, to = at(a, up(b), 1 - zl, 1), dev(a, down(b), zl)
        elif n < 11:
            src, to = at(a, across_b[n - 7], 0, 2), dev(up(a), b, zl)
        elif n < 15:
            src, to = at(a, across_b[n - 11], 0, 2), dev(down(a), b, zl)
        elif n < 19:
            src, to = at(down(a), across_b[n - 15], 0, 1), dev(up(a), b, zl)
        else:
            src, to = at(up(a), across_b[n - 19], 1, 1), dev(down(a), b, zl)
        return remote(src, src, gs.at[half, n], gr.at[half, n], (to, col))

    def sib_copy(half, g, j):
        a, b, _ = axes(half)
        aa = (a, down(a), up(a), across(a))[g]
        bb = (b, down(b), up(b), across(b))[j]
        src = lat.at[core * 2 + half, pl.ds((aa * 4 + bb) * 2, 2)]
        return remote(src, src, ss.at[half, g * 4 + j], sr.at[half, g * 4 + j], sibling)

    def out_copy(half, n):
        a, b, dev = axes(half)
        buf = wout.at[half]
        across_b = (b, down(b), up(b), across(b))
        if n <= 2:
            src = buf.at[a * 4 + b]
            to = dev(a, up(b) if n == 1 else down(b), zl)
        elif n == 3:
            src, to = buf.at[a * 4 + down(b), pl.ds(0, 64)], dev(a, up(b), zl)
        elif n == 4:
            src, to = buf.at[a * 4 + up(b), pl.ds(64, 64)], dev(a, down(b), zl)
        elif n < 9:
            src, to = buf.at[a * 4 + across_b[n - 5]], dev(up(a), b, zl)
        elif n < 13:
            src, to = buf.at[a * 4 + across_b[n - 9]], dev(down(a), b, zl)
        elif n < 17:
            src, to = buf.at[down(a) * 4 + across_b[n - 13], pl.ds(0, 64)], dev(up(a), b, zl)
        else:
            src, to = buf.at[up(a) * 4 + across_b[n - 17], pl.ds(64, 64)], dev(down(a), b, zl)
        return remote(src, src, os.at[half, n], orr.at[half, n], (to, col))

    def out_step(half, landed, sent):
        for n in landed:
            out_copy(half, n).wait_recv()
        for n in sent:
            out_copy(half, n).start()

    first_steps = {
        0: [((1,), (3, 6, 10)), ((2,), (4, 7, 11)), ((5,), (13,)), ((9,), (17,))],
        1: [((3, 4), (8, 12)), ((6,), (14,)), ((10,), (18,))],
        2: [((7,), (15,)), ((11,), (19,))],
        3: [((8,), (16,)), ((12,), (20,))],
    }
    second_steps = {
        0: [((), (1, 2, 5, 9))],
        1: [((1,), (3, 6, 10)), ((2,), (4, 7, 11))],
        2: [((5,), (13,)), ((9,), (17,))],
        3: [((3, 4), (8, 12)), ((6,), (14,)), ((10,), (18,))],
        4: [((7,), (15,)), ((11,), (19,))],
        5: [((8,), (16,)), ((12,), (20,))],
    }

    def out_stage(stage):
        if stage == 0:
            out_first.wait_recv()
        for steps, own in ((second_steps, False), (first_steps, True)):
            for half in (0, 1):

                @pl.when((zl == half) if own else (zl != half))
                def _(half=half, steps=steps):
                    for landed, sent in steps.get(stage, []):
                        out_step(half, landed, sent)

    own_out = wout.at[zl, jnp.where(zl == 0, x * 4 + y, y * 4 + x)]
    out_first = remote(wout_ref, own_out, os.at[0, 0], orr.at[0, 0], (row_of(x, y, 1 - zl), col))
    out_local = pltpu.make_async_copy(wout_ref, own_out, ls.at[3])

    lax.fori_loop(1, ROWS, small_start, 0)
    local_q = pltpu.make_async_copy(q_part(row), queries.at[row], ls.at[1])
    local_w = pltpu.make_async_copy(w_part(row), wkv.at[row], ls.at[2])
    local_q.start()
    local_w.start()
    out_local.start()
    out_local.wait()
    for half in (0, 1):

        @pl.when(zl == half)
        def _(half=half):
            for n in (1, 2, 5, 9):
                out_copy(half, n).start()

    @pl.when(core != home)
    def _():
        col_copy(0).wait_send()

    @pl.when(core == home)
    def _():
        own_piece.wait()

    def piece_arrival(slot):
        return remote(lat_ref, own_place, cs.at[0], cr.at[slot], sibling)

    for slot in range(4):

        @pl.when(jnp.logical_not((core == home) & (own_slot == slot)))
        def _(slot=slot):
            piece_arrival(slot).wait_recv()

    for half in (0, 1):
        for n in (0, 1, 2):
            lat_copy(half, n).start()
    for half in (0, 1):
        lat_copy(half, 0).wait_recv()
        for n in (3, 4, 7, 11):
            lat_copy(half, n).start()
        sib_copy(half, 0, 0).start()
    out_first.start()
    for half in (0, 1):
        lat_copy(half, 1).wait_recv()
        lat_copy(half, 5).start()
        lat_copy(half, 4).wait_recv()
        lat_copy(half, 6).start()
    for half in (0, 1):
        lat_copy(half, 3).wait_recv()
        for n in (8, 12):
            lat_copy(half, n).start()
        sib_copy(half, 0, 1).start()
        lat_copy(half, 2).wait_recv()
        for n in (9, 13):
            lat_copy(half, n).start()
        sib_copy(half, 0, 2).start()
    for half in (0, 1):
        lat_copy(half, 5).wait_recv()
        lat_copy(half, 6).wait_recv()
        for n in (10, 14):
            lat_copy(half, n).start()
        sib_copy(half, 0, 3).start()

    def small_wait(d, carry):
        w_copy(d).wait()
        q_copy(d).wait()
        return carry

    lax.fori_loop(1, ROWS, small_wait, 0)
    local_q.wait()
    local_w.wait()
    wkt[...] = wkv[...].reshape(512, 256).T
    values[:, HEAD:] = jnp.ones((ROWS * TOK, HEAD), BF16)

    for j in range(4):
        for half in (0, 1):
            lat_copy(half, 7 + j).wait_recv()
            lat_copy(half, 15 + j).start()
            sib_copy(half, 1, j).start()
            lat_copy(half, 11 + j).wait_recv()
            lat_copy(half, 19 + j).start()
            sib_copy(half, 2, j).start()
    for half in (0, 1):
        for g in range(3):
            for j in range(4):
                sib_copy(half, g, j).wait_recv()

    def project(i, carry):
        later = i - 9
        j = later // 2
        beyond = jnp.where(j == 0, 0, jnp.where(j == 1, 3, jnp.where(j == 2, 1, 2)))
        even = lax.rem(later + 10, 2) == 0
        xx = jnp.where(i < 9, x + lax.rem(i, 3) + 3, jnp.where(even, x + 2, x + beyond))
        yy = jnp.where(i < 9, y + i // 3 + 3, jnp.where(even, y + beyond, y + 2))
        xx = lax.rem(xx, 4)
        yy = lax.rem(yy, 4)
        for zz in (0, 1):
            first = (xx * 4 + yy) * 2 + zz
            second = (yy * 4 + xx) * 2 + zz
            tokens = jnp.concatenate(
                [lat[0, first], lat[1, second], lat[2, first], lat[3, second]], axis=0
            )
            at = pl.multiple_of(row_of(xx, yy, zz) * TOK, TOK)
            pair = jnp.dot(wkt[...], tokens, preferred_element_type=F32)
            keys_t[:, pl.ds(at, TOK)] = pair[:HEAD].astype(BF16)
            values[pl.ds(at, TOK), :HEAD] = pair[HEAD:].T.astype(BF16)
        return carry

    def last_group(j):
        for half in (0, 1):
            lat_copy(half, 15 + j).wait_recv()
            lat_copy(half, 19 + j).wait_recv()
            sib_copy(half, 3, j).start()

    lax.fori_loop(0, 3, project, 0)
    last_group(0)
    lax.fori_loop(3, 6, project, 0)
    last_group(1)
    out_stage(0)
    lax.fori_loop(6, 9, project, 0)

    def last_handed(j):
        for half in (0, 1):
            sib_copy(half, 3, j).wait_recv()

    last_handed(0)
    lax.fori_loop(9, 11, project, 0)
    last_group(2)
    last_handed(1)
    lax.fori_loop(11, 13, project, 0)
    last_group(3)
    last_handed(2)
    lax.fori_loop(13, 15, project, 0)
    last_handed(3)
    project(15, 0)

    att_place = feats.at[
        col,
        pl.ds(pl.multiple_of(row // 4 * STRIPE, STRIPE), STRIPE),
        pl.ds(pl.multiple_of(head_local * HEAD, HEAD), HEAD),
    ]

    def att_copy(r, d):
        return remote(att.at[r], att_place, hs.at[d], hr.at[d], (r, col))

    local_att = pltpu.make_async_copy(att.at[row], att_place, ls.at[4])

    def place_of(h, k):
        return h * 2 + k

    def feat_copy(n, part):
        lanes = pl.ds(pl.multiple_of(part * 256, 256), 256)

        def at(place, first, count):
            return feats.at[place, pl.ds(first, count), lanes]

        if n == 0:
            src, to = at(col, 0, TOK), place_of(up(zh), core)
        elif n == 1:
            src, to = at(col, 0, TOK), place_of(down(zh), core)
        elif n == 2:
            src, to = at(col, 0, TOK), place_of(zh, 1 - core)
        elif n == 3:
            src, to = at(place_of(down(zh), core), 0, 192), place_of(up(zh), core)
        elif n == 4:
            src, to = at(place_of(up(zh), core), 192, 192), place_of(down(zh), core)
        elif n == 5:
            src, to = at(place_of(down(zh), core), 0, TOK), place_of(zh, 1 - core)
        elif n == 6:
            src, to = at(place_of(up(zh), core), 0, TOK), place_of(zh, 1 - core)
        else:
            src, to = at(place_of(across(zh), core), 0, TOK), place_of(zh, 1 - core)
        return remote(src, src, zs.at[part, n], zr.at[part, n], (row, to))

    def feat_start(part):
        @pl.when(head_local // 2 == part)
        def _():
            local_att.start()

        def arrival(j, carry):
            source = j // 2 * 4 + part * 2 + lax.rem(j, 2)

            @pl.when(source != row)
            def _():
                att_copy(row, lax.rem(source - row + ROWS, ROWS)).wait_recv()

            return carry

        lax.fori_loop(0, ROWS // 2, arrival, 0)

        @pl.when(head_local // 2 == part)
        def _():
            local_att.wait()

        for n in range(3):
            feat_copy(n, part).start()

    def feat_forward(part):
        feat_copy(0, part).wait_recv()
        feat_copy(3, part).start()
        feat_copy(1, part).wait_recv()
        feat_copy(4, part).start()
        feat_copy(5, part).start()
        feat_copy(6, part).start()

    def feat_hand_over(part):
        feat_copy(3, part).wait_recv()
        feat_copy(4, part).wait_recv()
        feat_copy(7, part).start()

    turned = head_local // 2
    my_block = row // QROWS
    early = jnp.where(my_block == 3, 1, 0)

    def beside(tick):
        for after in range(1, 5):

            @pl.when(tick == after + 1)
            def _(after=after):
                out_stage(after)

        @pl.when(
            ((tick == 2) & (my_block == 0))
            | ((tick == 3) & (my_block == 1))
            | ((tick == 4) & (my_block == 3))
            | ((tick == 4) & (my_block == 2))
        )
        def _():
            feat_start(early)

        @pl.when((tick == 5) & (my_block == 0))
        def _():
            feat_forward(early)

        @pl.when(((tick == 4) & (my_block == 0)) | ((tick == 5) & (my_block == 1)))
        def _():
            feat_start(1 - early)

    def turn(query, start, first_key, keys, allowed):
        scores = jnp.dot(
            query[start:], keys_t[:, pl.ds(first_key, keys)], preferred_element_type=F32
        )
        if allowed is not None:
            scores = jnp.where(allowed, scores, NEG_FILL)
        before = top[start:, :1]
        now = jnp.maximum(before, jnp.max(scores, axis=1, keepdims=True))
        weights = jnp.exp2((scores - now) * SCALE).astype(BF16)
        rescale = jnp.exp2((before - now) * SCALE)
        acc[start:, :] = acc[start:, :] * rescale + jnp.dot(
            weights, values[pl.ds(first_key, keys), :], preferred_element_type=F32
        )
        top[start:, :] = jnp.broadcast_to(now, (QB - start, HEAD))

    def attend(turn_index, carry):
        block = lax.rem(turn_index + 3 * turned, BLOCKS)
        before = jnp.where(
            turned == 0,
            turn_index * (turn_index - 1) // 2,
            jnp.where(turn_index >= 2, turn_index + 1, 0),
        )
        query = queries[pl.ds(block * QROWS, QROWS)].reshape(QB, HEAD)
        acc[...] = jnp.zeros_like(acc)
        top[...] = jnp.full(top.shape, NEG_FILL, F32)

        def full(step, inner):
            beside(before + step)
            turn(query, 0, pl.multiple_of(step * KB, KB), KB, None)
            return inner

        lax.fori_loop(0, block, full, 0)
        for part in range(QROWS // DIAG):
            start = part * DIAG * STRIPE
            shape = (QB - start, DIAG * TOK)
            place = lax.broadcasted_iota(jnp.int32, shape, 0)
            key = lax.broadcasted_iota(jnp.int32, shape, 1)
            source = sum(
                (place >= STRIPE * j).astype(jnp.int32) for j in range(1, QROWS - part * DIAG)
            )
            position = source * (TOK - STRIPE) + place + row // 4 * STRIPE
            first_key = pl.multiple_of(block * KB + part * DIAG * TOK, DIAG * TOK)
            turn(query, start, first_key, DIAG * TOK, key <= position)
        done = (acc[:, :HEAD] / acc[:, HEAD:]).astype(BF16)
        att[pl.ds(block * QROWS, QROWS)] = done.reshape(QROWS, STRIPE, HEAD)
        for j in range(QROWS):
            r = block * QROWS + j

            @pl.when(r != row)
            def _(r=r):
                att_copy(r, lax.rem(row - r + ROWS, ROWS)).start()

        return carry

    lax.fori_loop(0, BLOCKS, attend, 0)

    @pl.when(my_block >= 2)
    def _():
        feat_start(1 - early)

    out_stage(5)

    @pl.when(my_block != 0)
    def _():
        feat_forward(early)

    feat_forward(1 - early)
    feat_hand_over(early)
    for half in (0, 1):
        for n in range(13, 21):
            out_copy(half, n).wait_recv()

    def mix(c, part, first=False):
        low = c // 4
        within = lax.rem(c, 4)
        weights = []
        for j in (0, 1):
            xx = part * 2 + j
            weights.append(wout[low, jnp.where(low == 0, xx * 4 + within, within * 4 + xx)])
        heads = feats[c, :, pl.ds(pl.multiple_of(part * 256, 256), 256)]
        product = jnp.dot(heads, jnp.concatenate(weights, axis=0), preferred_element_type=F32)
        if first:
            total[...] = product
        else:
            total[...] += product

    def mix_some(n, part):
        h = jnp.where(n == 0, zh, jnp.where(lax.rem(n, 2) == 1, down(zh), up(zh)))
        k = jnp.where((n == 1) | (n == 2), core, 1 - core)
        mix(place_of(h, k), part)
        return part

    mix(col, early, True)
    for part in (early, 1 - early):
        if part is not early:
            mix(col, part)
        feat_copy(2, part).wait_recv()
        lax.fori_loop(0, 3, mix_some, part)
        feat_copy(5, part).wait_recv()
        feat_copy(6, part).wait_recv()
        lax.fori_loop(3, 5, mix_some, part)
        if part is not early:
            feat_hand_over(part)
        mix(place_of(across(zh), core), part)
        feat_copy(7, part).wait_recv()
        mix(place_of(across(zh), 1 - core), part)
    out_ref[...] = total[...].astype(BF16)

    for d in (1, 2, 3):
        col_copy(d).wait_send()
    for half in (0, 1):
        for n in range(23):
            lat_copy(half, n).wait_send()
        for g in range(4):
            for j in range(4):
                sib_copy(half, g, j).wait_send()
        for n in range(1, 21):
            out_copy(half, n).wait_send()
    out_first.wait_send()

    def att_sent(d, carry):
        att_copy(lax.rem(row - d + ROWS, ROWS), d).wait_send()
        return carry

    lax.fori_loop(1, ROWS, att_sent, 0)
    for part in (0, 1):
        for n in range(8):
            feat_copy(n, part).wait_send()


def per_device(latent, w_kv, queries, w_out):
    dma = pltpu.SemaphoreType.DMA
    vmem = pltpu.VMEM
    return pl.pallas_call(
        kernel,
        out_shape=jax.ShapeDtypeStruct((TOK, w_out.shape[1]), BF16),
        in_specs=[pl.BlockSpec(memory_space=pltpu.VMEM)] * 4,
        out_specs=pl.BlockSpec(memory_space=pltpu.VMEM),
        scratch_shapes=[
            vmem((4, ROWS, 128, TOK), BF16),
            vmem((ROWS, 16, 256), BF16),
            vmem((256, 512), BF16),
            vmem((ROWS, STRIPE, HEAD), BF16),
            vmem((HEAD, ROWS * TOK), BF16),
            vmem((ROWS * TOK, 256), BF16),
            vmem((ROWS, STRIPE, HEAD), BF16),
            vmem((8, TOK, 512), BF16),
            vmem((2, 16, 128, 896), BF16),
            vmem((QB, 256), F32),
            vmem((QB, 128), F32),
            vmem((TOK, 896), F32),
            dma((4,)), dma((4,)),
            dma((ROWS,)), dma((ROWS,)),
            dma((ROWS,)), dma((ROWS,)),
            dma((2, 23)), dma((2, 23)),
            dma((2, 16)), dma((2, 16)),
            dma((2, 21)), dma((2, 21)),
            dma((ROWS,)), dma((ROWS,)),
            dma((2, 8)), dma((2, 8)),
            dma((5,)),
        ],
        compiler_params=pltpu.CompilerParams(
            collective_id=0, has_side_effects=True, vmem_limit_bytes=60 * 1024 * 1024
        ),
        cost_estimate=pl.CostEstimate(
            flops=12_000_000_000, bytes_accessed=2_000_000, transcendentals=11_000_000
        ),
    )(latent.T, w_kv, queries, w_out)


def solution(mesh):
    spec = P("row", "col")
    return jax.shard_map(
        per_device, mesh=mesh, in_specs=(spec,) * 4, out_specs=spec, check_vma=False
    )
```
